32 devices in a mesh: groups: 2 (over y), ep: 4 (over z), half: 2 (over x), tp: 2 (over core).
Axes of the slice: x: 2, y: 2, z: 4, core: 2. Of those that a mesh axis runs over, the one named last changes fastest.
Arguments:
- queries: bfloat16 [512, 2048], P(('groups', 'ep', 'half'), 'tp'), parts along dimension 0, may hold values from -6 to 6
- new_keys: bfloat16 [512, 256], P(('groups', 'ep', 'half'), 'tp'), parts along dimension 0, may hold values from -4 to 4
- new_values: bfloat16 [512, 256], P(('groups', 'ep', 'half'), 'tp'), parts along dimension 0, may hold values from -4 to 4
- cache_keys: bfloat16 [512, 2, 64, 128], P(('groups', 'ep', 'half'), 'tp'), parts along dimension 0, may hold values from -4 to 4
- cache_values: bfloat16 [512, 2, 64, 128], P(('groups', 'ep', 'half'), 'tp'), parts along dimension 0, may hold values from -4 to 4
- lengths: int32 [512], P(('groups', 'ep', 'half')), parts along dimension 0, may hold values from 1 to 64, as said below
- out_weight: bfloat16 [2048, 2048], P('tp', 'half'), may hold values from -0.375 to 0.375
- residual: bfloat16 [512, 2048], P(('groups', 'ep'), 'half'), parts along dimension 0, may hold values from -5 to 5
- norm_gain: float32 [2048], P('half'), may hold values from 0.1 to 1.9
- expert_ids: int32 [512, 8], P(('groups', 'ep')), parts along dimension 0, may hold values from 0 to 63, all different within a row; in each aligned block of 64 rows (0 to 63, 64 to 127, ...) at most 12 rows name the same one
- gate_weights: float32 [512, 8], P(('groups', 'ep')), parts along dimension 0, may hold values from 0.05 to 1
- w_gate: bfloat16 [64, 768, 2048], P(('ep', 'tp'), 'half'), may hold values from -0.125 to 0.125
- w_up: bfloat16 [64, 768, 2048], P(('ep', 'tp'), 'half'), may hold values from -0.125 to 0.125
- w_down: bfloat16 [64, 768, 2048], P(('ep', 'tp'), 'half'), may hold values from -0.625 to 0.625
Outputs:
- layer_out: bfloat16 [512, 2048], P(('groups', 'ep'), ('half', 'tp')), parts along dimension 0
The draws below stay inside these ranges and needn't reach their ends.
There are 2 independent parts, one for each index of `groups`. The reference program is written for one: setup_inputs(seed, part) draws one part's arguments, and reference() takes and returns one part's arrays. A program takes and returns all parts, laid end to end along the dimension named above; an argument that names none is the same for every part. Nothing has to cross between parts.
Inputs may be any that keep to these rules, and one draw needn't show every extreme that they name: `expert_ids`: in each block of 64 consecutive rows (the tokens of one index of ep) no expert is named by more than 12 rows. `lengths`: among each device's 32 requests one has 64 cached tokens.
All inputs are finite; a program needn't handle non-finite values.
Results may differ from the reference program's by a relative error of at most 0.014.
Values may be sent and summed in bfloat16 or wider, within the bound.
A program may use at most 128 MiB of HBM per device.

```python
import math
import jax
import jax.numpy as jnp
import numpy as np
from jax import lax

D = 2048
HEADS = 16
KVH = 2
HD = 128
FF = 768
EXPERTS = 64
TOPK = 8
REQ_DEV = 32
CTX = 64
GROUP = 8
TOK_EP = 64
REQS = 256
CAP = 12
N_EP = 4
N_HALF = 2


def draw_queries(key, part):
    values = jnp.clip(jax.random.normal(jax.random.fold_in(key, 102), (REQS, HEADS, HD)), -4.0, 4.0)
    return values.reshape(REQS, HEADS * HD).astype(jnp.bfloat16)


def draw_cache_keys(key, part):
    values = jnp.clip(jax.random.normal(jax.random.fold_in(key, 104), (REQS, KVH, CTX, HD)), -4.0, 4.0)
    return values.astype(jnp.bfloat16)


def draw_lengths(key, part):
    drawn = jax.random.randint(jax.random.fold_in(key, 111), (REQS,), 1, CTX + 1)
    offsets = jax.random.randint(jax.random.fold_in(key, 112), (REQS // REQ_DEV,), 0, REQ_DEV)
    longest = (jnp.arange(REQ_DEV)[None, :] == offsets[:, None]).reshape(REQS)
    return jnp.where(longest, CTX, drawn).astype(jnp.int32)


def levels(rng, shape, cuts, smallest, high):
    level = 1.0
    for dim, shards_of in cuts:
        heights = jax.random.uniform(jax.random.fold_in(jax.random.fold_in(rng, 6), dim), (shards_of,), jnp.float32, smallest / len(cuts), high / len(cuts))
        level = level * jnp.repeat(jnp.exp(heights), shape[dim] // shards_of).reshape((-1,) + (1,) * (len(shape) - 1 - dim))
    return level


def shared_out(own_key, own, number, rows, number_of, top, reach, slope):
    sequence = jax.random.permutation(own_key, number_of)
    heavy_load, usual = shares(number_of, rows * top, reach, slope, True), shares(number_of, rows * top, reach, slope, False)
    places = jnp.arange(number_of)

    def named(sizes, offset_by):
        used = int((sizes > 0).sum())
        fixed = max(1, used // 4)
        passed = fixed + (places - fixed + offset_by * (used - fixed)) % max(1, number_of - fixed)
        return jnp.zeros((number_of,), jnp.int32).at[sequence[jnp.where(places < fixed, places, passed)]].set(jnp.asarray(sizes, jnp.int32))

    sizes = jnp.where(number % 4 == 0, named(heavy_load, number // 4), named(usual, number - number // 4 - 1))
    mixed = jax.random.permutation(jax.random.fold_in(own, 3), number_of)
    donor, sink = mixed[0:number_of // 2 * 2:2], mixed[1:number_of // 2 * 2:2]
    room = jnp.minimum(sizes[donor] - 1, reach - sizes[sink]) // 2
    room = jnp.where((donor == sequence[0]) | (sink == sequence[0]) | (sizes[sink] == 0), 0, jnp.maximum(room, 0))
    passed = jax.random.randint(jax.random.fold_in(own, 4), (number_of // 2,), 0, 1 << 20) % (room + 1)
    sizes = sizes.at[donor].add(-passed).at[sink].add(passed)
    labels = jnp.searchsorted(jnp.cumsum(sizes), jnp.arange(rows * top), side="right").astype(jnp.int32)
    listing = labels.reshape(top, rows).T
    listing = listing[jax.random.permutation(jax.random.fold_in(own, 1), rows)]
    offset_by = jax.random.randint(jax.random.fold_in(own, 2), (rows, 1), 0, top)
    return jnp.take_along_axis(listing, (jnp.arange(top)[None, :] + offset_by) % top, axis=1)


def shares(number_of, total, reach, slope, full):
    loads = [(1 << 20) // math.isqrt(standing ** slope) + 1 for standing in range(1, number_of + 1)]
    largest = reach if full else min(reach, max(-(-total // number_of), total * loads[0] // sum(loads)))
    least = 1 if total - largest >= number_of - 1 else 0
    counts, surplus = [largest] + [least] * (number_of - 1), total - largest - least * (number_of - 1)
    while surplus > 0:
        candidates = [i for i in range(1, number_of) if counts[i] < largest] or [i for i in range(1, number_of) if counts[i] < reach]
        whole, budget = sum([loads[i] for i in candidates]), surplus
        for i in candidates:
            addition = min(reach - counts[i], max(1, budget * loads[i] // whole), surplus)
            counts[i] = counts[i] + addition
            surplus = surplus - addition
    return np.array(counts)


def normal_values(rng, extent, deviation, limit, cuts=(), kind=jnp.bfloat16):
    entries = jax.random.normal(rng, extent, jnp.float32) * deviation
    if len(cuts) > 0:
        entries = levels(rng, extent, cuts, -0.22, 0.18) * entries
    return jnp.clip(entries, min=-limit, max=limit).astype(kind)


def setup_inputs(seed: int = 0, part: int = 0) -> dict:
    key_list = jax.random.split(jax.random.key(seed), 15)
    part_keys = jax.random.split(jax.random.fold_in(key_list[14], part), 15)
    queries = draw_queries(jax.random.fold_in(jax.random.fold_in(key_list[14], part), 71), part)
    new_keys = normal_values(part_keys[1], (REQS, KVH * HD), 1.0, 4.0, ((0, 8), (1, 2)))
    new_values = normal_values(part_keys[2], (REQS, KVH * HD), 1.0, 4.0, ((0, 8), (1, 2)))
    cache_keys = draw_cache_keys(jax.random.fold_in(jax.random.fold_in(key_list[14], part), 71), part)
    cache_values = normal_values(part_keys[4], (REQS, KVH, CTX, HD), 1.0, 4.0, ((0, 8), (1, 2)))
    lengths = draw_lengths(jax.random.fold_in(jax.random.fold_in(key_list[14], part), 71), part)
    out_weight = normal_values(key_list[6], (HEADS * HD, D), (HEADS * HD // 8) ** -0.5, 0.375, ((0, 2), (1, 2)))
    residual = normal_values(part_keys[7], (REQS, D), 1.0, 5.0, ((0, 4), (1, 2)))
    norm_gain = jnp.clip(1.0 + 0.18 * jax.random.normal(key_list[8], (D,), jnp.float32), 0.1, 1.9)
    expert_ids_keys = jax.random.split(jax.random.fold_in(part_keys[9], 1), REQS // TOK_EP)
    expert_ids_turns = jax.random.permutation(jax.random.fold_in(part_keys[9], 3), REQS // TOK_EP)
    expert_ids = jax.vmap(lambda own, number: shared_out(jax.random.fold_in(part_keys[9], 2), own, number, TOK_EP, EXPERTS, TOPK, CAP, 2))(expert_ids_keys, expert_ids_turns).reshape((REQS, TOPK))
    gate_weights = jnp.clip(0.05 + 0.95 * jax.random.uniform(part_keys[10], (REQS, TOPK), jnp.float32) ** levels(part_keys[10], (REQS, TOPK), ((0, 4),), -0.2, 0.2), 0.05, 1.0)
    w_gate = normal_values(key_list[11], (EXPERTS, FF, D), D ** -0.5, 0.125, ((0, 8), (1, 2)))
    w_up = normal_values(key_list[12], (EXPERTS, FF, D), D ** -0.5, 0.125, ((0, 8), (1, 2)))
    w_down = normal_values(key_list[13], (EXPERTS, FF, D), (FF // 8) ** -0.5, 0.625, ((0, 8), (1, 2)))
    return dict(queries=queries, new_keys=new_keys, new_values=new_values, cache_keys=cache_keys, cache_values=cache_values, lengths=lengths, out_weight=out_weight, residual=residual, norm_gain=norm_gain, expert_ids=expert_ids, gate_weights=gate_weights, w_gate=w_gate, w_up=w_up, w_down=w_down)


def attention(queries, new_keys, new_values, cache_keys, cache_values, lengths):
    query_blocks = queries.reshape(REQS, KVH, GROUP, HD).astype(jnp.float32)
    score_scale = 1.0 / math.sqrt(HD)
    scores = jnp.einsum('rkgd,rkcd->rkgc', query_blocks, cache_keys.astype(jnp.float32)) * score_scale
    own_score = jnp.einsum('rkgd,rkd->rkg', query_blocks, new_keys.reshape(REQS, KVH, HD).astype(jnp.float32)) * score_scale
    valid = lax.iota(jnp.int32, CTX)[None, :] < lengths[:, None]
    scores = jnp.where(valid[:, None, None, :], scores, -1e+30)
    highest = jnp.maximum(lax.optimization_barrier(jnp.max(scores, axis=-1)), own_score)
    weights = jnp.exp(scores - highest[..., None])
    own_weight = jnp.exp(own_score - highest)
    denominator = lax.optimization_barrier(jnp.sum(weights, axis=-1)) + own_weight
    probs = (weights / denominator[..., None]).astype(jnp.bfloat16)
    own_prob = (own_weight / denominator).astype(jnp.bfloat16)
    mixture = jnp.einsum('rkgc,rkcd->rkgd', probs.astype(jnp.float32), cache_values.astype(jnp.float32))
    mixture = mixture + own_prob.astype(jnp.float32)[..., None] * new_values.reshape(REQS, KVH, 1, HD).astype(jnp.float32)
    return mixture.astype(jnp.bfloat16).reshape(REQS, HEADS * HD)

def reference(queries, new_keys, new_values, cache_keys, cache_values, lengths, out_weight, residual, norm_gain, expert_ids, gate_weights, w_gate, w_up, w_down):
    attended = attention(queries, new_keys, new_values, cache_keys, cache_values, lengths)
    mixed = jnp.dot(attended, out_weight, preferred_element_type=jnp.float32)
    hidden = residual.astype(jnp.float32) + mixed
    inverse = lax.rsqrt(lax.optimization_barrier(jnp.mean(hidden * hidden, axis=1)) + 1e-06)
    normed = (hidden * inverse[:, None] * norm_gain[None, :]).astype(jnp.bfloat16)
    gates = gate_weights / lax.optimization_barrier(jnp.sum(gate_weights, axis=1, keepdims=True))
    id_blocks = expert_ids.reshape(N_EP, TOK_EP * TOPK)
    one_hot = (id_blocks[:, :, None] == jnp.arange(EXPERTS, dtype=jnp.int32)[None, None, :]).astype(jnp.int32)
    earlier = jnp.cumsum(one_hot, axis=1) - one_hot
    slot = lax.optimization_barrier(jnp.sum(earlier * one_hot, axis=2)).astype(jnp.int32)
    block_index = jnp.broadcast_to(jnp.arange(N_EP, dtype=jnp.int32)[:, None], slot.shape)
    token_index = block_index * TOK_EP + (jnp.arange(TOK_EP * TOPK, dtype=jnp.int32) // TOPK)[None, :]
    table = jnp.full((EXPERTS, N_EP, CAP), REQS, jnp.int32).at[id_blocks, block_index, slot].set(token_index)
    gate_table = jnp.zeros((EXPERTS, N_EP, CAP), jnp.float32).at[id_blocks, block_index, slot].set(gates.reshape(N_EP, TOK_EP * TOPK))
    padded = jnp.concatenate([normed, jnp.zeros((1, D), jnp.bfloat16)], axis=0)
    block_width = FF // N_HALF

    def expert_step(carry, pieces):
        rows_index, row_gates, gate_matrix, up_matrix, down_matrix = pieces
        flat_index = rows_index.reshape(-1)
        rows = padded[flat_index].astype(jnp.float32)
        gate_part = jnp.dot(rows, gate_matrix.astype(jnp.float32).T, precision=lax.Precision.HIGHEST)
        up_part = jnp.dot(rows, up_matrix.astype(jnp.float32).T, precision=lax.Precision.HIGHEST)
        activation = (jax.nn.silu(gate_part) * up_part).astype(jnp.bfloat16).astype(jnp.float32)
        summed = jnp.zeros((rows.shape[0], D), jnp.float32)
        for block in range(N_HALF):
            lower = block * block_width
            part = jnp.dot(activation[:, lower:lower + block_width], down_matrix[lower:lower + block_width].astype(jnp.float32), precision=lax.Precision.HIGHEST)
            part = lax.optimization_barrier(part.astype(jnp.bfloat16))
            summed = summed + part.astype(jnp.float32)
        carry = carry.at[flat_index].add(row_gates.reshape(-1)[:, None] * summed)
        return (carry, None)
    start_sum = jnp.zeros((REQS + 1, D), jnp.float32)
    combined, unused = lax.scan(expert_step, start_sum, (table, gate_table, w_gate, w_up, w_down))
    return (hidden + combined[:REQS]).astype(jnp.bfloat16)
```

```python
import functools
import math

import jax
import jax.numpy as jnp
from jax import lax
from jax.experimental import pallas as pl
from jax.experimental.pallas import tpu as pltpu
from jax.sharding import PartitionSpec as P

EXPERTS = 64


EPSILON = 1e-06


def attend(queries, new_keys, new_values, cache_keys, cache_values, lengths):
    requests, key_heads, context, head_size = cache_keys.shape
    sharing = queries.shape[1] // (key_heads * head_size)
    query_blocks = queries.reshape(requests, key_heads, sharing, head_size)
    score_scale = 1.0 / math.sqrt(head_size)
    scores = (
        jnp.einsum("rkgd,rkcd->rkgc", query_blocks, cache_keys, preferred_element_type=jnp.float32)
        * score_scale
    )
    own_score = (
        jnp.einsum(
            "rkgd,rkd->rkg",
            query_blocks,
            new_keys.reshape(requests, key_heads, head_size),
            preferred_element_type=jnp.float32,
        )
        * score_scale
    )
    valid = lax.iota(jnp.int32, context)[None, :] < lengths[:, None]
    scores = jnp.where(valid[:, None, None, :], scores, -1e30)
    highest = jnp.maximum(jnp.max(scores, axis=-1), own_score)
    weights = jnp.exp(scores - highest[..., None])
    own_weight = jnp.exp(own_score - highest)
    denominator = jnp.sum(weights, axis=-1) + own_weight
    probs = (weights / denominator[..., None]).astype(jnp.bfloat16)
    own_prob = (own_weight / denominator).astype(jnp.bfloat16)
    mixture = jnp.einsum("rkgc,rkcd->rkgd", probs, cache_values, preferred_element_type=jnp.float32)
    mixture = mixture + own_prob.astype(jnp.float32)[..., None] * new_values.reshape(
        requests, key_heads, 1, head_size
    ).astype(jnp.float32)
    return mixture.astype(jnp.bfloat16).reshape(requests, key_heads * sharing * head_size)


def combine_rows(returned_rows, target, gates):
    token_rows, top_count = target.shape
    safe_target = jnp.maximum(target, 0).reshape(-1)
    picked = jnp.take(returned_rows, safe_target, axis=0).reshape(
        token_rows, top_count, returned_rows.shape[1]
    )
    weighting = jnp.where(target >= 0, gates, 0.0)
    return jnp.sum(picked.astype(jnp.float32) * weighting[..., None], axis=1)


def staged(
    queries,
    new_keys,
    new_values,
    cache_keys,
    cache_values,
    lengths,
    out_weight,
    residual,
    norm_gain,
    expert_ids,
    gate_weights,
    w_gate,
    w_up,
    w_down,
):
    attended = attend(queries, new_keys, new_values, cache_keys, cache_values, lengths)
    partial_mix = jnp.dot(
        lax.all_gather(attended, "half", axis=0, tiled=True),
        out_weight,
        preferred_element_type=jnp.float32,
    )
    mixed = lax.psum(partial_mix.astype(jnp.bfloat16), "tp").astype(jnp.float32)
    hidden = residual.astype(jnp.float32) + mixed
    squares = lax.psum(jnp.sum(hidden * hidden, axis=1), "half")
    half_width = hidden.shape[1]
    width = half_width * lax.axis_size("half")
    normed = (hidden * lax.rsqrt(squares / width + EPSILON)[:, None] * norm_gain[None, :]).astype(
        jnp.bfloat16
    )
    token_rows, top_count = expert_ids.shape
    ep_count = lax.axis_size("ep")
    tp_count = lax.axis_size("tp")
    local_experts = w_gate.shape[0]
    capacity = token_rows * top_count * 3 // (2 * EXPERTS)
    slot_count = ep_count * local_experts * capacity
    flat_ids = expert_ids.reshape(-1)
    one_hot = (flat_ids[:, None] == lax.iota(jnp.int32, EXPERTS)[None, :]).astype(jnp.int32)
    earlier = jnp.cumsum(one_hot, axis=0) - one_hot
    slot = jnp.sum(earlier * one_hot, axis=1)
    owner_ep = flat_ids // (local_experts * tp_count)
    owner_tp = flat_ids // local_experts % tp_count
    target = owner_ep * (local_experts * capacity) + flat_ids % local_experts * capacity + slot
    target = jnp.where(owner_tp == lax.axis_index("tp"), target, -1).reshape(token_rows, top_count)
    dispatch_matrix = jnp.any(
        lax.iota(jnp.int32, slot_count)[:, None, None] == target[None, :, :], axis=2
    ).astype(jnp.bfloat16)
    gates = gate_weights / jnp.sum(gate_weights, axis=1, keepdims=True)
    full_rows = lax.all_gather(normed, "half", axis=1, tiled=True)
    outgoing = jnp.dot(dispatch_matrix, full_rows, preferred_element_type=jnp.float32).astype(
        jnp.bfloat16
    )
    arrived = lax.all_to_all(
        outgoing.reshape(ep_count, local_experts, capacity, width),
        "ep",
        split_axis=0,
        concat_axis=0,
        tiled=True,
    )
    gate_part = jnp.einsum("secd,efd->secf", arrived, w_gate, preferred_element_type=jnp.float32)
    up_part = jnp.einsum("secd,efd->secf", arrived, w_up, preferred_element_type=jnp.float32)
    activation = (jax.nn.silu(gate_part) * up_part).astype(jnp.bfloat16)
    expert_out = jnp.einsum(
        "secf,efd->secd", activation, w_down, preferred_element_type=jnp.float32
    ).astype(jnp.bfloat16)
    summed = lax.psum_scatter(
        expert_out.astype(jnp.float32).astype(jnp.bfloat16), "half", scatter_dimension=3, tiled=True
    ).astype(jnp.float32)
    returned = lax.all_to_all(
        summed.reshape(ep_count, local_experts * capacity, half_width).astype(jnp.bfloat16),
        "ep",
        split_axis=0,
        concat_axis=0,
        tiled=True,
    ).astype(jnp.float32)
    term = combine_rows(returned.reshape(slot_count, half_width), target, gates)
    expert_sum = lax.psum_scatter(
        term.astype(jnp.bfloat16), "tp", scatter_dimension=1, tiled=True
    ).astype(jnp.float32)
    slice_width = expert_sum.shape[1]
    own_columns = lax.dynamic_slice_in_dim(
        hidden, lax.axis_index("tp") * slice_width, slice_width, 1
    )
    return (own_columns + expert_sum).astype(jnp.bfloat16)


VMEM_BYTES = 60 * 1024 * 1024
LANES = 128
ROW_TILE = 8
MESH = pl.DeviceIdType.MESH


def remote(src, dst, send, recv, **where):
    return pltpu.make_async_remote_copy(
        src_ref=src,
        dst_ref=dst,
        send_sem=send,
        recv_sem=recv,
        device_id=where,
        device_id_type=MESH,
    )


def layer_kernel(
    sizes,
    q_ref,
    nk_ref,
    nv_ref,
    len_ref,
    res_ref,
    gain_ref,
    ids_ref,
    gw_ref,
    ck_hbm,
    cv_hbm,
    ow_hbm,
    wg_hbm,
    wu_hbm,
    wd_hbm,
    out_ref,
    ck,
    cv,
    ow,
    wg,
    wu,
    wd,
    att_f,
    att,
    gain,
    table,
    mix_out,
    mix_in,
    own_hidden,
    hid,
    xg,
    squares,
    act,
    a_out,
    a_in,
    mine,
    b_out,
    b_in,
    kept,
    c_out,
    c_in,
    load_sem,
    w_sem,
    att_s,
    att_r,
    gain_s,
    gain_r,
    table_s,
    table_r,
    mix_s,
    mix_r,
    hz_s,
    hz_r,
    hx_s,
    hx_r,
    ht_s,
    ht_r,
    a_s,
    a_r,
    b_s,
    b_r,
    c_s,
    c_r,
):
    n_ep, n_half = sizes["ep"], sizes["half"]
    me_z, me_h, me_t = lax.axis_index("ep"), lax.axis_index("half"), lax.axis_index("tp")
    other = 1 - me_t
    requests, context, head_size = ck.shape
    heads = q_ref.shape[1] // head_size
    local, hidden_units = wg.shape[0], wg.shape[1]
    block, piece = res_ref.shape[0], res_ref.shape[1] // 2
    rows = n_ep * block
    width = n_half * 2 * piece

    loads = [
        pltpu.make_async_copy(ck_hbm, ck, load_sem.at[0]),
        pltpu.make_async_copy(cv_hbm, cv, load_sem.at[1]),
        pltpu.make_async_copy(ow_hbm, ow, load_sem.at[2]),
    ]
    for load in loads:
        load.start()

    def weight_copy(k, j):
        if k < 2:
            return pltpu.make_async_copy(
                (wg_hbm, wu_hbm)[k].at[j], (wg, wu)[k].at[j], w_sem.at[k, j]
            )
        part = pl.ds(j * hidden_units, hidden_units)
        return pltpu.make_async_copy(wd_hbm.at[part], wd.at[part], w_sem.at[k, j])

    for j in range(local):
        weight_copy(0, j).start()
        weight_copy(1, j).start()
    for j in range(local):
        weight_copy(2, j).start()

    barrier = pltpu.get_barrier_semaphore()
    pl.semaphore_signal(barrier, inc=1, device_id={"tp": other}, device_id_type=MESH)
    for d in range(1, n_half):
        pl.semaphore_signal(
            barrier, inc=1, device_id={"half": lax.rem(me_h + d, n_half)}, device_id_type=MESH
        )
    for d in range(1, n_ep):
        pl.semaphore_signal(
            barrier, inc=1, device_id={"ep": lax.rem(me_z + d, n_ep)}, device_id_type=MESH
        )

    sent = []

    def go(copy):
        copy.start()
        sent.append(copy)
        return copy

    gates = gw_ref[...] / jnp.sum(gw_ref[...], axis=1, keepdims=True)
    expert_lane = lax.broadcasted_iota(jnp.int32, (block, table.shape[2]), 1)
    own_table = jnp.zeros((block, table.shape[2]), jnp.float32)
    for k in range(ids_ref.shape[1]):
        own_table += jnp.where(expert_lane == ids_ref[:, k : k + 1], gates[:, k : k + 1], 0.0)
    table[me_z] = own_table
    gain[me_h] = jnp.broadcast_to(gain_ref[...], gain.shape[1:])

    pl.semaphore_wait(barrier, 1 + (n_half - 1) + (n_ep - 1))

    gain_copies = [
        go(
            remote(
                gain.at[me_h],
                gain.at[me_h],
                gain_s.at[d],
                gain_r.at[d],
                half=lax.rem(me_h + d, n_half),
            )
        )
        for d in range(1, n_half)
    ]
    table_copies = [
        go(
            remote(
                table.at[me_z],
                table.at[me_z],
                table_s.at[d],
                table_r.at[d],
                ep=lax.rem(me_z + d, n_ep),
            )
        )
        for d in range(1, n_ep)
    ]

    loads[0].wait()
    loads[1].wait()
    step = ROW_TILE
    scale = 1.0 / math.sqrt(head_size)
    shape = (heads * step, step * context)
    row = lax.broadcasted_iota(jnp.int32, shape, 0)
    column = lax.broadcasted_iota(jnp.int32, shape, 1)
    same = (row % step) == (column // context)
    position = column % context
    for g in range(requests // step):
        part = pl.ds(g * step, step)
        q_all = q_ref[part].astype(jnp.float32)
        q = jnp.concatenate(
            [q_all[:, h * head_size : (h + 1) * head_size] for h in range(heads)], axis=0
        )
        nk = jnp.concatenate([nk_ref[part].astype(jnp.float32)] * heads, axis=0)
        nv = jnp.concatenate([nv_ref[part].astype(jnp.float32)] * heads, axis=0)
        valid = jnp.concatenate([len_ref[part]] * heads, axis=0)
        keys = ck[part].reshape(step * context, head_size)
        values = cv[part].reshape(step * context, head_size)
        scores = (
            lax.dot_general(
                q.astype(jnp.bfloat16),
                keys,
                (((1,), (1,)), ((), ())),
                preferred_element_type=jnp.float32,
            )
            * scale
        )
        own = jnp.sum(q * nk, axis=1, keepdims=True) * scale
        scores = jnp.where(same & (position < valid), scores, -1e30)
        highest = jnp.maximum(jnp.max(scores, axis=1, keepdims=True), own)
        weights = jnp.exp(scores - highest)
        own_weight = jnp.exp(own - highest)
        inverse = 1.0 / (jnp.sum(weights, axis=1, keepdims=True) + own_weight)
        probs = (weights * inverse).astype(jnp.bfloat16)
        own_prob = (own_weight * inverse).astype(jnp.bfloat16).astype(jnp.float32)
        mixture = jnp.dot(probs, values, preferred_element_type=jnp.float32) + own_prob * nv
        for h in range(heads):
            att_f[part, h * head_size : (h + 1) * head_size] = mixture[h * step : (h + 1) * step]
    att[me_h] = att_f[...].astype(jnp.bfloat16)
    att_copies = [
        go(
            remote(
                att.at[me_h],
                att.at[me_h],
                att_s.at[d],
                att_r.at[d],
                half=lax.rem(me_h + d, n_half),
            )
        )
        for d in range(1, n_half)
    ]
    loads[2].wait()
    for copy in att_copies:
        copy.wait_recv()

    attended = att[...].reshape(block, att.shape[2])
    other_columns = pl.ds(pl.multiple_of(other * piece, piece), piece)
    my_columns = pl.ds(pl.multiple_of(me_t * piece, piece), piece)
    mix_out[...] = jnp.dot(
        attended, ow[:, other_columns], preferred_element_type=jnp.float32
    ).astype(jnp.bfloat16)
    mix_copy = go(remote(mix_out, mix_in, mix_s, mix_r, tp=other))
    mixed = jnp.dot(attended, ow[:, my_columns], preferred_element_type=jnp.float32)
    mixed = mixed + res_ref[:, my_columns].astype(jnp.float32)
    mix_copy.wait_recv()
    hidden = mixed + mix_in[...].astype(jnp.float32)
    own_hidden[...] = hidden
    hid[me_z, me_h, me_t] = hidden.astype(jnp.bfloat16)

    z_copies = {
        d: go(
            remote(
                hid.at[me_z, me_h, me_t],
                hid.at[me_z, me_h, me_t],
                hz_s.at[d],
                hz_r.at[d],
                ep=lax.rem(me_z + d, n_ep),
            )
        )
        for d in range(1, n_ep)
    }
    for copy in gain_copies:
        copy.wait_recv()
    squares[...] = jnp.zeros_like(squares)

    def take(z, h, t):
        value = hid[z, h, t].astype(jnp.float32)
        square = value * value
        total = square[:, :LANES]
        for k in range(1, piece // LANES):
            total = total + square[:, k * LANES : (k + 1) * LANES]
        squares[z] += total
        columns = pl.ds(pl.multiple_of((h * 2 + t) * piece, piece), piece)
        gain_columns = pl.ds(pl.multiple_of(t * piece, piece), piece)
        xg[pl.ds(pl.multiple_of(z * block, block), block), columns] = (
            value * gain[h, 0:1, gain_columns]
        ).astype(jnp.bfloat16)

    x_copies, t_copies = {}, {}
    for d in range(n_ep):
        z = lax.rem(me_z - d + n_ep, n_ep)
        if d > 0:
            z_copies[d].wait_recv()
        here = hid.at[z, me_h, me_t]
        for dx in range(1, n_half):
            x_copies[d, dx] = go(
                remote(
                    here,
                    here,
                    hx_s.at[dx, d],
                    hx_r.at[dx, d],
                    half=lax.rem(me_h + dx, n_half),
                )
            )
        t_copies[d, 0] = go(remote(here, here, ht_s.at[0, d], ht_r.at[0, d], tp=other))
        take(z, me_h, me_t)
    for d in range(n_ep):
        z = lax.rem(me_z - d + n_ep, n_ep)
        for dx in range(1, n_half):
            h = lax.rem(me_h - dx + n_half, n_half)
            x_copies[d, dx].wait_recv()
            here = hid.at[z, h, me_t]
            t_copies[d, dx] = go(remote(here, here, ht_s.at[dx, d], ht_r.at[dx, d], tp=other))
            take(z, h, me_t)
    for dx in range(n_half):
        for d in range(n_ep):
            z = lax.rem(me_z - d + n_ep, n_ep)
            h = lax.rem(me_h - dx + n_half, n_half)
            t_copies[d, dx].wait_recv()
            take(z, h, other)
    for copy in table_copies:
        copy.wait_recv()

    total = jnp.sum(squares[...].reshape(rows, LANES), axis=1, keepdims=True)
    inverse = lax.rsqrt(total / width + EPSILON)
    lane = lax.broadcasted_iota(jnp.int32, (rows, table.shape[2]), 1)
    first = (me_z * 2 + me_t) * local

    def expert(j, carry):
        weight_copy(0, j).wait()
        weight_copy(1, j).wait()
        normed = xg[...]
        contract = (((1,), (1,)), ((), ()))
        gate = lax.dot_general(normed, wg[j], contract, preferred_element_type=jnp.float32)
        up = lax.dot_general(normed, wu[j], contract, preferred_element_type=jnp.float32)
        weight = jnp.sum(
            jnp.where(lane == first + j, table[...].reshape(rows, table.shape[2]), 0.0),
            axis=1,
            keepdims=True,
        )
        gate = gate * inverse
        silu = gate / (1.0 + jnp.exp(jnp.minimum(-gate, 88.0)))
        act[:, pl.ds(pl.multiple_of(j * hidden_units, hidden_units), hidden_units)] = (
            silu * (up * (inverse * weight))
        ).astype(jnp.bfloat16)
        return carry

    lax.fori_loop(0, local, expert, 0)
    for j in range(local):
        weight_copy(2, j).wait()

    def down(h, t):
        columns = pl.ds(pl.multiple_of((h * 2 + t) * piece, piece), piece)
        return jnp.dot(act[...], wd[:, columns], preferred_element_type=jnp.float32)

    b_copies = {}
    for dx in [*range(1, n_half), 0]:
        h = lax.rem(me_h + dx, n_half)
        a_out[dx] = down(h, other).astype(jnp.bfloat16)
        a_copy = go(remote(a_out.at[dx], a_in.at[dx], a_s.at[dx], a_r.at[dx], tp=other))
        mine[...] = down(h, me_t)
        a_copy.wait_recv()
        if dx > 0:
            b_out[dx] = (mine[...] + a_in[dx].astype(jnp.float32)).astype(jnp.bfloat16)
            for d in [*range(1, n_ep), 0]:
                z = lax.rem(me_z + d, n_ep)
                part = pl.ds(pl.multiple_of(z * block, block), block)
                b_copies[dx, d] = go(
                    remote(
                        b_out.at[dx, part],
                        b_in.at[dx, part],
                        b_s.at[dx, d],
                        b_r.at[dx, d],
                        half=h,
                    )
                )
        else:
            kept[...] = mine[...] + a_in[dx].astype(jnp.float32)
    c_copies = {}
    for d in [*range(1, n_ep), 0]:
        z = lax.rem(me_z + d, n_ep)
        part = pl.ds(pl.multiple_of(z * block, block), block)
        total = kept[part]
        for dx in range(1, n_half):
            b_copies[dx, d].wait_recv()
            total = total + b_in[dx, part].astype(jnp.float32)
        if d > 0:
            c_out[d] = total.astype(jnp.bfloat16)
            c_copies[d] = go(remote(c_out.at[d], c_in.at[d], c_s.at[d], c_r.at[d], ep=z))
        else:
            own_hidden[...] += total
    result = own_hidden[...]
    for d in range(1, n_ep):
        c_copies[d].wait_recv()
        result = result + c_in[d].astype(jnp.float32)
    out_ref[...] = result.astype(jnp.bfloat16)
    for copy in sent:
        copy.wait_send()


def on_device(sizes, *args):
    (
        queries,
        new_keys,
        new_values,
        cache_keys,
        cache_values,
        lengths,
        out_weight,
        residual,
        norm_gain,
        expert_ids,
        gate_weights,
        w_gate,
        w_up,
        w_down,
    ) = args
    n_ep, n_half, n_tp = sizes["ep"], sizes["half"], sizes["tp"]
    requests, key_heads, context, head_size = cache_keys.shape
    block, half_width = residual.shape
    local, hidden_units, width = w_gate.shape
    piece = half_width // 2
    rows = n_ep * block
    lanes = -(-(local * n_ep * n_tp) // LANES) * LANES
    bf16, f32 = jnp.bfloat16, jnp.float32
    buffers = [
        ((requests, context, head_size), bf16),
        ((requests, context, head_size), bf16),
        (out_weight.shape, bf16),
        (w_gate.shape, bf16),
        (w_up.shape, bf16),
        ((local * hidden_units, width), bf16),
        (queries.shape, f32),
        ((n_half,) + queries.shape, bf16),
        ((n_half, ROW_TILE, half_width), f32),
        ((n_ep, block, lanes), f32),
        ((block, piece), bf16),
        ((block, piece), bf16),
        ((block, piece), f32),
        ((n_ep, n_half, n_tp, block, piece), bf16),
        ((rows, width), bf16),
        ((n_ep, block, LANES), f32),
        ((rows, local * hidden_units), bf16),
        ((n_half, rows, piece), bf16),
        ((n_half, rows, piece), bf16),
        ((rows, piece), f32),
        ((n_half, rows, piece), bf16),
        ((n_half, rows, piece), bf16),
        ((rows, piece), f32),
        ((n_ep, block, piece), bf16),
        ((n_ep, block, piece), bf16),
    ]
    held = sum(math.prod(shape) * jnp.dtype(kind).itemsize for shape, kind in buffers)
    fits = (
        held * 5 // 4 < VMEM_BYTES
        and n_tp == 2
        and key_heads == 1
        and hidden_units % LANES == 0
        and piece % LANES == 0
        and requests % (2 * ROW_TILE) == 0
        and block == n_half * requests
    )
    if not fits:
        return staged(*args)
    dma = pltpu.SemaphoreType.DMA
    semaphores = [
        dma((3,)),
        dma((3, local)),
        dma((n_half,)),
        dma((n_half,)),
        dma((n_half,)),
        dma((n_half,)),
        dma((n_ep,)),
        dma((n_ep,)),
        dma,
        dma,
        dma((n_ep,)),
        dma((n_ep,)),
        dma((n_half, n_ep)),
        dma((n_half, n_ep)),
        dma((n_half, n_ep)),
        dma((n_half, n_ep)),
        dma((n_half,)),
        dma((n_half,)),
        dma((n_half, n_ep)),
        dma((n_half, n_ep)),
        dma((n_ep,)),
        dma((n_ep,)),
    ]
    vmem = pl.BlockSpec(memory_space=pltpu.VMEM)
    hbm = pl.BlockSpec(memory_space=pl.ANY)
    return pl.pallas_call(
        functools.partial(layer_kernel, dict(ep=n_ep, half=n_half)),
        out_shape=jax.ShapeDtypeStruct((block, piece), bf16),
        in_specs=[vmem] * 8 + [hbm] * 6,
        out_specs=vmem,
        scratch_shapes=[pltpu.VMEM(shape, kind) for shape, kind in buffers] + semaphores,
        compiler_params=pltpu.CompilerParams(
            collective_id=0, has_side_effects=True, vmem_limit_bytes=VMEM_BYTES
        ),
    )(
        queries,
        new_keys,
        new_values,
        lengths.reshape(requests, 1),
        residual,
        norm_gain.reshape(1, half_width),
        expert_ids,
        gate_weights,
        cache_keys.reshape(requests, context, head_size),
        cache_values.reshape(requests, context, head_size),
        out_weight,
        w_gate,
        w_up,
        w_down.reshape(local * hidden_units, width),
    )


def solution(mesh):
    placed = (
        P(("groups", "ep", "half"), "tp"),
        P(("groups", "ep", "half"), "tp"),
        P(("groups", "ep", "half"), "tp"),
        P(("groups", "ep", "half"), "tp", None, None),
        P(("groups", "ep", "half"), "tp", None, None),
        P(("groups", "ep", "half")),
        P("tp", "half"),
        P(("groups", "ep"), "half"),
        P("half"),
        P(("groups", "ep"), None),
        P(("groups", "ep"), None),
        P(("ep", "tp"), "half", None),
        P(("ep", "tp"), "half", None),
        P(("ep", "tp"), "half", None),
    )
    return jax.shard_map(
        functools.partial(on_device, mesh.shape),
        mesh=mesh,
        in_specs=placed,
        out_specs=P(("groups", "ep"), ("half", "tp")),
        check_vma=False,
    )
```

```python
import functools
import math

import jax
import jax.numpy as jnp
from jax import lax
from jax.experimental import pallas as pl
from jax.experimental.pallas import tpu as pltpu
from jax.sharding import PartitionSpec as P

EXPERTS = 64


EPSILON = 1e-06


def attend(queries, new_keys, new_values, cache_keys, cache_values, lengths):
    requests, key_heads, context, head_size = cache_keys.shape
    sharing = queries.shape[1] // (key_heads * head_size)
    query_blocks = queries.reshape(requests, key_heads, sharing, head_size)
    score_scale = 1.0 / math.sqrt(head_size)
    scores = (
        jnp.einsum("rkgd,rkcd->rkgc", query_blocks, cache_keys, preferred_element_type=jnp.float32)
        * score_scale
    )
    own_score = (
        jnp.einsum(
            "rkgd,rkd->rkg",
            query_blocks,
            new_keys.reshape(requests, key_heads, head_size),
            preferred_element_type=jnp.float32,
        )
        * score_scale
    )
    valid = lax.iota(jnp.int32, context)[None, :] < lengths[:, None]
    scores = jnp.where(valid[:, None, None, :], scores, -1e30)
    highest = jnp.maximum(jnp.max(scores, axis=-1), own_score)
    weights = jnp.exp(scores - highest[..., None])
    own_weight = jnp.exp(own_score - highest)
    denominator = jnp.sum(weights, axis=-1) + own_weight
    probs = (weights / denominator[..., None]).astype(jnp.bfloat16)
    own_prob = (own_weight / denominator).astype(jnp.bfloat16)
    mixture = jnp.einsum("rkgc,rkcd->rkgd", probs, cache_values, preferred_element_type=jnp.float32)
    mixture = mixture + own_prob.astype(jnp.float32)[..., None] * new_values.reshape(
        requests, key_heads, 1, head_size
    ).astype(jnp.float32)
    return mixture.astype(jnp.bfloat16).reshape(requests, key_heads * sharing * head_size)


def combine_rows(returned_rows, target, gates):
    token_rows, top_count = target.shape
    safe_target = jnp.maximum(target, 0).reshape(-1)
    picked = jnp.take(returned_rows, safe_target, axis=0).reshape(
        token_rows, top_count, returned_rows.shape[1]
    )
    weighting = jnp.where(target >= 0, gates, 0.0)
    return jnp.sum(picked.astype(jnp.float32) * weighting[..., None], axis=1)


def staged(
    queries,
    new_keys,
    new_values,
    cache_keys,
    cache_values,
    lengths,
    out_weight,
    residual,
    norm_gain,
    expert_ids,
    gate_weights,
    w_gate,
    w_up,
    w_down,
):
    attended = attend(queries, new_keys, new_values, cache_keys, cache_values, lengths)
    partial_mix = jnp.dot(
        lax.all_gather(attended, "half", axis=0, tiled=True),
        out_weight,
        preferred_element_type=jnp.float32,
    )
    mixed = lax.psum(partial_mix.astype(jnp.bfloat16), "tp").astype(jnp.float32)
    hidden = residual.astype(jnp.float32) + mixed
    squares = lax.psum(jnp.sum(hidden * hidden, axis=1), "half")
    half_width = hidden.shape[1]
    width = half_width * lax.axis_size("half")
    normed = (hidden * lax.rsqrt(squares / width + EPSILON)[:, None] * norm_gain[None, :]).astype(
        jnp.bfloat16
    )
    token_rows, top_count = expert_ids.shape
    ep_count = lax.axis_size("ep")
    tp_count = lax.axis_size("tp")
    local_experts = w_gate.shape[0]
    capacity = token_rows * top_count * 3 // (2 * EXPERTS)
    slot_count = ep_count * local_experts * capacity
    flat_ids = expert_ids.reshape(-1)
    one_hot = (flat_ids[:, None] == lax.iota(jnp.int32, EXPERTS)[None, :]).astype(jnp.int32)
    earlier = jnp.cumsum(one_hot, axis=0) - one_hot
    slot = jnp.sum(earlier * one_hot, axis=1)
    owner_ep = flat_ids // (local_experts * tp_count)
    owner_tp = flat_ids // local_experts % tp_count
    target = owner_ep * (local_experts * capacity) + flat_ids % local_experts * capacity + slot
    target = jnp.where(owner_tp == lax.axis_index("tp"), target, -1).reshape(token_rows, top_count)
    dispatch_matrix = jnp.any(
        lax.iota(jnp.int32, slot_count)[:, None, None] == target[None, :, :], axis=2
    ).astype(jnp.bfloat16)
    gates = gate_weights / jnp.sum(gate_weights, axis=1, keepdims=True)
    full_rows = lax.all_gather(normed, "half", axis=1, tiled=True)
    outgoing = jnp.dot(dispatch_matrix, full_rows, preferred_element_type=jnp.float32).astype(
        jnp.bfloat16
    )
    arrived = lax.all_to_all(
        outgoing.reshape(ep_count, local_experts, capacity, width),
        "ep",
        split_axis=0,
        concat_axis=0,
        tiled=True,
    )
    gate_part = jnp.einsum("secd,efd->secf", arrived, w_gate, preferred_element_type=jnp.float32)
    up_part = jnp.einsum("secd,efd->secf", arrived, w_up, preferred_element_type=jnp.float32)
    activation = (jax.nn.silu(gate_part) * up_part).astype(jnp.bfloat16)
    expert_out = jnp.einsum(
        "secf,efd->secd", activation, w_down, preferred_element_type=jnp.float32
    ).astype(jnp.bfloat16)
    summed = lax.psum_scatter(
        expert_out.astype(jnp.float32).astype(jnp.bfloat16), "half", scatter_dimension=3, tiled=True
    ).astype(jnp.float32)
    returned = lax.all_to_all(
        summed.reshape(ep_count, local_experts * capacity, half_width).astype(jnp.bfloat16),
        "ep",
        split_axis=0,
        concat_axis=0,
        tiled=True,
    ).astype(jnp.float32)
    term = combine_rows(returned.reshape(slot_count, half_width), target, gates)
    expert_sum = lax.psum_scatter(
        term.astype(jnp.bfloat16), "tp", scatter_dimension=1, tiled=True
    ).astype(jnp.float32)
    slice_width = expert_sum.shape[1]
    own_columns = lax.dynamic_slice_in_dim(
        hidden, lax.axis_index("tp") * slice_width, slice_width, 1
    )
    return (own_columns + expert_sum).astype(jnp.bfloat16)


VMEM_BYTES = 60 * 1024 * 1024
LANES = 128
ROW_TILE = 8
MESH = pl.DeviceIdType.MESH


def remote(src, dst, send, recv, **where):
    return pltpu.make_async_remote_copy(
        src_ref=src,
        dst_ref=dst,
        send_sem=send,
        recv_sem=recv,
        device_id=where,
        device_id_type=MESH,
    )


def partner(index, p):
    bit = 1
    while bit <= p:
        if p & bit:
            index = index + bit - 2 * bit * (index // bit % 2)
        bit *= 2
    return index


def span_of(span):
    return pl.ds(span.start, span.stop - span.start)


def layer_kernel(
    sizes,
    q_ref,
    nk_ref,
    nv_ref,
    len_ref,
    res_ref,
    gain_ref,
    ids_ref,
    gw_ref,
    ck_hbm,
    cv_hbm,
    ow_hbm,
    wg_hbm,
    wu_hbm,
    wd_hbm,
    out_ref,
    ck,
    cv,
    ow,
    wgu,
    wd,
    att_f,
    att,
    gain,
    table,
    mix_out,
    mix_in,
    own_hidden,
    hid,
    xg,
    squares,
    act,
    a_out,
    a_in,
    b_out,
    b_in,
    kept,
    c_out,
    c_in,
    load_sem,
    w_sem,
    att_s,
    att_r,
    gain_s,
    gain_r,
    table_s,
    table_r,
    mix_s,
    mix_r,
    hz_s,
    hz_r,
    hx_s,
    hx_r,
    ht_s,
    ht_r,
    a_s,
    a_r,
    b_s,
    b_r,
    c_s,
    c_r,
):
    n_ep, n_half = sizes["ep"], sizes["half"]
    me_z, me_h, me_t = lax.axis_index("ep"), lax.axis_index("half"), lax.axis_index("tp")
    other = 1 - me_t
    requests, context, head_size = ck.shape
    heads = q_ref.shape[1] // head_size
    local, hidden_units = wgu.shape[0], wgu.shape[1] // 2
    block, piece = res_ref.shape[0], res_ref.shape[1] // 2
    rows = n_ep * block
    width = n_half * 2 * piece

    loads = [
        pltpu.make_async_copy(ck_hbm, ck, load_sem.at[0]),
        pltpu.make_async_copy(cv_hbm, cv, load_sem.at[1]),
        pltpu.make_async_copy(ow_hbm, ow, load_sem.at[2]),
    ]
    for load in loads:
        load.start()

    def weight_copy(k, j):
        if k < 2:
            return pltpu.make_async_copy(
                (wg_hbm, wu_hbm)[k].at[j],
                wgu.at[j, pl.ds(k * hidden_units, hidden_units)],
                w_sem.at[k, j],
            )
        part = pl.ds(j * hidden_units, hidden_units)
        return pltpu.make_async_copy(wd_hbm.at[part], wd.at[part], w_sem.at[k, j])

    for j in range(local):
        weight_copy(0, j).start()
        weight_copy(1, j).start()
    for j in range(local):
        weight_copy(2, j).start()

    barrier = pltpu.get_barrier_semaphore()
    pl.semaphore_signal(barrier, inc=1, device_id={"tp": other}, device_id_type=MESH)
    for d in range(1, n_half):
        pl.semaphore_signal(
            barrier, inc=1, device_id={"half": lax.rem(me_h + d, n_half)}, device_id_type=MESH
        )
    for p in range(1, n_ep):
        pl.semaphore_signal(barrier, inc=1, device_id={"ep": partner(me_z, p)}, device_id_type=MESH)

    sent = []

    def go(copy):
        copy.start()
        sent.append(copy)
        return copy

    spread = jnp.broadcast_to(len_ref[...].astype(jnp.float32), (LANES, requests)).T

    loads[0].wait()
    loads[1].wait()
    step = ROW_TILE
    scale = 1.0 / math.sqrt(head_size)
    shape = (heads * step, step * context)
    row = lax.broadcasted_iota(jnp.int32, shape, 0)
    column = lax.broadcasted_iota(jnp.int32, shape, 1)
    same = (row % step) == (column // context)
    position = (column % context).astype(jnp.float32)
    for g in range(requests // step):
        part = pl.ds(g * step, step)
        q_all = q_ref[part].astype(jnp.float32)
        q = jnp.concatenate(
            [q_all[:, h * head_size : (h + 1) * head_size] for h in range(heads)], axis=0
        )
        nk = jnp.concatenate([nk_ref[part].astype(jnp.float32)] * heads, axis=0)
        nv = jnp.concatenate([nv_ref[part].astype(jnp.float32)] * heads, axis=0)
        valid = jnp.concatenate([spread[g * step : (g + 1) * step, :1]] * heads, axis=0)
        keys = ck[part].reshape(step * context, head_size)
        values = cv[part].reshape(step * context, head_size)
        scores = (
            lax.dot_general(
                q.astype(jnp.bfloat16),
                keys,
                (((1,), (1,)), ((), ())),
                preferred_element_type=jnp.float32,
            )
            * scale
        )
        own = jnp.sum(q * nk, axis=1, keepdims=True) * scale
        scores = jnp.where(same & (position < valid), scores, -1e30)
        highest = jnp.maximum(jnp.max(scores, axis=1, keepdims=True), own)
        weights = jnp.exp(scores - highest)
        own_weight = jnp.exp(own - highest)
        inverse = 1.0 / (jnp.sum(weights, axis=1, keepdims=True) + own_weight)
        probs = (weights * inverse).astype(jnp.bfloat16)
        own_prob = (own_weight * inverse).astype(jnp.bfloat16).astype(jnp.float32)
        mixture = jnp.dot(probs, values, preferred_element_type=jnp.float32) + own_prob * nv
        for h in range(heads):
            att_f[part, h * head_size : (h + 1) * head_size] = mixture[h * step : (h + 1) * step]
    att[me_h] = att_f[...].astype(jnp.bfloat16)
    gates = gw_ref[...] / jnp.sum(gw_ref[...], axis=0, keepdims=True)
    expert_row = lax.broadcasted_iota(jnp.int32, (table.shape[2], block), 0)
    own_table = jnp.zeros((table.shape[2], block), jnp.float32)
    for k in range(ids_ref.shape[0]):
        own_table += jnp.where(expert_row == ids_ref[k : k + 1, :], gates[k : k + 1, :], 0.0)
    table[0] = own_table.T
    gain[me_h] = jnp.broadcast_to(gain_ref[...], gain.shape[1:])

    pl.semaphore_wait(barrier, 1 + (n_half - 1) + (n_ep - 1))
    att_copies = [
        go(
            remote(
                att.at[me_h],
                att.at[me_h],
                att_s.at[d],
                att_r.at[d],
                half=lax.rem(me_h + d, n_half),
            )
        )
        for d in range(1, n_half)
    ]
    gain_copies = [
        go(
            remote(
                gain.at[me_h],
                gain.at[me_h],
                gain_s.at[d],
                gain_r.at[d],
                half=lax.rem(me_h + d, n_half),
            )
        )
        for d in range(1, n_half)
    ]
    table_copies = [
        go(
            remote(
                table.at[0], table.at[p], table_s.at[p], table_r.at[p], ep=partner(me_z, p)
            )
        )
        for p in range(1, n_ep)
    ]
    loads[2].wait()
    for copy in att_copies:
        copy.wait_recv()

    attended = att[...].reshape(block, att.shape[2])
    other_columns = pl.ds(pl.multiple_of(other * piece, piece), piece)
    my_columns = pl.ds(pl.multiple_of(me_t * piece, piece), piece)
    mix_out[...] = jnp.dot(
        attended, ow[:, other_columns], preferred_element_type=jnp.float32
    ).astype(jnp.bfloat16)
    mix_copy = go(remote(mix_out, mix_in, mix_s, mix_r, tp=other))
    mixed = jnp.dot(attended, ow[:, my_columns], preferred_element_type=jnp.float32)
    mixed = mixed + res_ref[:, my_columns].astype(jnp.float32)
    mix_copy.wait_recv()
    hidden = mixed + mix_in[...].astype(jnp.float32)
    own_hidden[...] = hidden
    hid[0, me_h, me_t] = hidden.astype(jnp.bfloat16)

    z_copies = {
        p: go(
            remote(
                hid.at[0, me_h, me_t],
                hid.at[p, me_h, me_t],
                hz_s.at[p],
                hz_r.at[p],
                ep=partner(me_z, p),
            )
        )
        for p in range(1, n_ep)
    }
    x_copies, t_copies = {}, {}

    def take(p, h, t):
        value = hid[p, h, t].astype(jnp.float32)
        square = value * value
        total = square[:, :LANES]
        for k in range(1, piece // LANES):
            total = total + square[:, k * LANES : (k + 1) * LANES]
        squares[p] += total
        columns = pl.ds(pl.multiple_of((h * 2 + t) * piece, piece), piece)
        gain_columns = pl.ds(pl.multiple_of(t * piece, piece), piece)
        xg[p * block : (p + 1) * block, columns] = (value * gain[h, 0:1, gain_columns]).astype(
            jnp.bfloat16
        )

    def to_sibling(p, dx, h):
        here = hid.at[p, h, me_t]
        t_copies[p, dx] = go(remote(here, here, ht_s.at[dx, p], ht_r.at[dx, p], tp=other))

    def spread_own(group):
        for p in group:
            if p > 0:
                z_copies[p].wait_recv()
            here = hid.at[p, me_h, me_t]
            for dx in range(1, n_half):
                x_copies[p, dx] = go(
                    remote(
                        here,
                        here,
                        hx_s.at[dx, p],
                        hx_r.at[dx, p],
                        half=lax.rem(me_h + dx, n_half),
                    )
                )
            to_sibling(p, 0, me_h)

    def spread_crossed(group):
        for p in group:
            for dx in range(1, n_half):
                x_copies[p, dx].wait_recv()
                to_sibling(p, dx, lax.rem(me_h - dx + n_half, n_half))

    def take_all(group):
        for dx in range(n_half):
            for p in group:
                h = lax.rem(me_h - dx + n_half, n_half)
                take(p, h, me_t)
                t_copies[p, dx].wait_recv()
                take(p, h, other)

    near, far = range(n_ep // 2), range(n_ep // 2, n_ep)
    group_rows = rows // 2
    lane = lax.broadcasted_iota(jnp.int32, (group_rows, table.shape[2]), 1)
    first = (me_z * 2 + me_t) * local

    def experts(group, low, high, load):
        span = slice(group[0] * block, group[0] * block + group_rows)
        blocks = slice(group[0], group[0] + len(group))
        total = jnp.sum(
            squares[blocks].reshape(group_rows, LANES), axis=1, keepdims=True
        )
        inverse = lax.rsqrt(total / width + EPSILON)

        def expert(j, carry):
            if load:
                weight_copy(0, j).wait()
                weight_copy(1, j).wait()
            both = lax.dot_general(
                xg[span], wgu[j], (((1,), (1,)), ((), ())), preferred_element_type=jnp.float32
            )
            weight = jnp.sum(
                jnp.where(
                    lane == first + j,
                    table[blocks].reshape(group_rows, table.shape[2]),
                    0.0,
                ),
                axis=1,
                keepdims=True,
            )
            gate = both[:, :hidden_units] * inverse
            silu = gate / (1.0 + jnp.exp(jnp.minimum(-gate, 88.0)))
            act[span, pl.ds(pl.multiple_of(j * hidden_units, hidden_units), hidden_units)] = (
                silu * (both[:, hidden_units:] * (inverse * weight))
            ).astype(jnp.bfloat16)
            return carry

        lax.fori_loop(low, high, expert, 0)

    b_copies, c_copies = {}, {}

    def down(group):
        span = slice(group[0] * block, group[0] * block + group_rows)
        order = [*range(1, n_half), 0]

        def columns_of(h, t):
            columns = pl.ds(pl.multiple_of((h * 2 + t) * piece, piece), piece)
            return jnp.dot(act[span], wd[:, columns], preferred_element_type=jnp.float32)

        side = group[0] // len(group)
        a_copies = {}
        for dx in order:
            h = lax.rem(me_h + dx, n_half)
            a_out[dx, span] = columns_of(h, other).astype(jnp.bfloat16)
            a_copies[dx] = go(
                remote(
                    a_out.at[dx, span_of(span)],
                    a_in.at[dx, span_of(span)],
                    a_s.at[dx, side],
                    a_r.at[dx, side],
                    tp=other,
                )
            )
        for dx in order:
            h = lax.rem(me_h + dx, n_half)
            kept[span] = columns_of(h, me_t)
            a_copies[dx].wait_recv()
            total = kept[span] + a_in[dx, span].astype(jnp.float32)
            if dx == 0:
                kept[span] = total
                continue
            b_out[dx, span] = total.astype(jnp.bfloat16)
            for p in reversed(group):
                part = pl.ds(p * block, block)
                b_copies[p, dx] = go(
                    remote(
                        b_out.at[dx, part],
                        b_in.at[dx, part],
                        b_s.at[dx, p],
                        b_r.at[dx, p],
                        half=h,
                    )
                )

    def send_back(group):
        for p in reversed(group):
            part = slice(p * block, (p + 1) * block)
            total = kept[part]
            for dx in range(1, n_half):
                b_copies[p, dx].wait_recv()
                total = total + b_in[dx, part].astype(jnp.float32)
            if p > 0:
                c_out[p] = total.astype(jnp.bfloat16)
                c_copies[p] = go(
                    remote(c_out.at[p], c_in.at[p], c_s.at[p], c_r.at[p], ep=partner(me_z, p))
                )
            else:
                own_hidden[...] += total

    spread_own(near)
    for copy in gain_copies:
        copy.wait_recv()
    squares[...] = jnp.zeros_like(squares)
    spread_crossed(near)
    for copy in table_copies:
        copy.wait_recv()
    take_all(near)
    cuts = [0, local // 4, local * 5 // 8, local]
    experts(near, cuts[0], cuts[1], True)
    spread_own(far)
    experts(near, cuts[1], cuts[2], True)
    spread_crossed(far)
    experts(near, cuts[2], cuts[3], True)
    for j in range(local):
        weight_copy(2, j).wait()
    down(near)
    take_all(far)
    experts(far, 0, local, False)
    send_back(near)
    down(far)
    send_back(far)
    result = own_hidden[...]
    for p in range(1, n_ep):
        c_copies[p].wait_recv()
        result = result + c_in[p].astype(jnp.float32)
    out_ref[...] = result.astype(jnp.bfloat16)
    for copy in sent:
        copy.wait_send()


def on_device(sizes, *args):
    (
        queries,
        new_keys,
        new_values,
        cache_keys,
        cache_values,
        lengths,
        out_weight,
        residual,
        norm_gain,
        expert_ids,
        gate_weights,
        w_gate,
        w_up,
        w_down,
    ) = args
    n_ep, n_half, n_tp = sizes["ep"], sizes["half"], sizes["tp"]
    requests, key_heads, context, head_size = cache_keys.shape
    block, half_width = residual.shape
    local, hidden_units, width = w_gate.shape
    piece = half_width // 2
    rows = n_ep * block
    lanes = -(-(local * n_ep * n_tp) // LANES) * LANES
    bf16, f32 = jnp.bfloat16, jnp.float32
    buffers = [
        ((requests, context, head_size), bf16),
        ((requests, context, head_size), bf16),
        (out_weight.shape, bf16),
        ((local, 2 * hidden_units, width), bf16),
        ((local * hidden_units, width), bf16),
        (queries.shape, f32),
        ((n_half,) + queries.shape, bf16),
        ((n_half, ROW_TILE, half_width), f32),
        ((n_ep, block, lanes), f32),
        ((block, piece), bf16),
        ((block, piece), bf16),
        ((block, piece), f32),
        ((n_ep, n_half, n_tp, block, piece), bf16),
        ((rows, width), bf16),
        ((n_ep, block, LANES), f32),
        ((rows, local * hidden_units), bf16),
        ((n_half, rows, piece), bf16),
        ((n_half, rows, piece), bf16),
        ((n_half, rows, piece), bf16),
        ((n_half, rows, piece), bf16),
        ((rows, piece), f32),
        ((n_ep, block, piece), bf16),
        ((n_ep, block, piece), bf16),
    ]
    held = sum(math.prod(shape) * jnp.dtype(kind).itemsize for shape, kind in buffers)
    fits = (
        held * 5 // 4 < VMEM_BYTES
        and n_tp == 2
        and n_ep > 1
        and n_ep & (n_ep - 1) == 0
        and key_heads == 1
        and hidden_units % LANES == 0
        and piece % LANES == 0
        and requests % (2 * ROW_TILE) == 0
        and block == n_half * requests
    )
    if not fits:
        return staged(*args)
    dma = pltpu.SemaphoreType.DMA
    semaphores = [
        dma((3,)),
        dma((3, local)),
        dma((n_half,)),
        dma((n_half,)),
        dma((n_half,)),
        dma((n_half,)),
        dma((n_ep,)),
        dma((n_ep,)),
        dma,
        dma,
        dma((n_ep,)),
        dma((n_ep,)),
        dma((n_half, n_ep)),
        dma((n_half, n_ep)),
        dma((n_half, n_ep)),
        dma((n_half, n_ep)),
        dma((n_half, 2)),
        dma((n_half, 2)),
        dma((n_half, n_ep)),
        dma((n_half, n_ep)),
        dma((n_ep,)),
        dma((n_ep,)),
    ]
    vmem = pl.BlockSpec(memory_space=pltpu.VMEM)
    hbm = pl.BlockSpec(memory_space=pl.ANY)
    return pl.pallas_call(
        functools.partial(layer_kernel, dict(ep=n_ep, half=n_half)),
        out_shape=jax.ShapeDtypeStruct((block, piece), bf16),
        in_specs=[vmem] * 8 + [hbm] * 6,
        out_specs=vmem,
        scratch_shapes=[pltpu.VMEM(shape, kind) for shape, kind in buffers] + semaphores,
        compiler_params=pltpu.CompilerParams(
            collective_id=0, has_side_effects=True, vmem_limit_bytes=VMEM_BYTES
        ),
    )(
        queries,
        new_keys,
        new_values,
        lengths.reshape(1, requests),
        residual,
        norm_gain.reshape(1, half_width),
        expert_ids.T,
        gate_weights.T,
        cache_keys.reshape(requests, context, head_size),
        cache_values.reshape(requests, context, head_size),
        out_weight,
        w_gate,
        w_up,
        w_down.reshape(local * hidden_units, width),
    )


def solution(mesh):
    placed = (
        P(("groups", "ep", "half"), "tp"),
        P(("groups", "ep", "half"), "tp"),
        P(("groups", "ep", "half"), "tp"),
        P(("groups", "ep", "half"), "tp", None, None),
        P(("groups", "ep", "half"), "tp", None, None),
        P(("groups", "ep", "half")),
        P("tp", "half"),
        P(("groups", "ep"), "half"),
        P("half"),
        P(("groups", "ep"), None),
        P(("groups", "ep"), None),
        P(("ep", "tp"), "half", None),
        P(("ep", "tp"), "half", None),
        P(("ep", "tp"), "half", None),
    )
    return jax.shard_map(
        functools.partial(on_device, mesh.shape),
        mesh=mesh,
        in_specs=placed,
        out_specs=P(("groups", "ep"), ("half", "tp")),
        check_vma=False,
    )
```

```python
import functools
import math

import jax
import jax.numpy as jnp
from jax import lax
from jax.experimental import pallas as pl
from jax.experimental.pallas import tpu as pltpu
from jax.sharding import PartitionSpec as P

EXPERTS = 64


EPSILON = 1e-06


def attend(queries, new_keys, new_values, cache_keys, cache_values, lengths):
    requests, key_heads, context, head_size = cache_keys.shape
    sharing = queries.shape[1] // (key_heads * head_size)
    query_blocks = queries.reshape(requests, key_heads, sharing, head_size)
    score_scale = 1.0 / math.sqrt(head_size)
    scores = (
        jnp.einsum("rkgd,rkcd->rkgc", query_blocks, cache_keys, preferred_element_type=jnp.float32)
        * score_scale
    )
    own_score = (
        jnp.einsum(
            "rkgd,rkd->rkg",
            query_blocks,
            new_keys.reshape(requests, key_heads, head_size),
            preferred_element_type=jnp.float32,
        )
        * score_scale
    )
    valid = lax.iota(jnp.int32, context)[None, :] < lengths[:, None]
    scores = jnp.where(valid[:, None, None, :], scores, -1e30)
    highest = jnp.maximum(jnp.max(scores, axis=-1), own_score)
    weights = jnp.exp(scores - highest[..., None])
    own_weight = jnp.exp(own_score - highest)
    denominator = jnp.sum(weights, axis=-1) + own_weight
    probs = (weights / denominator[..., None]).astype(jnp.bfloat16)
    own_prob = (own_weight / denominator).astype(jnp.bfloat16)
    mixture = jnp.einsum("rkgc,rkcd->rkgd", probs, cache_values, preferred_element_type=jnp.float32)
    mixture = mixture + own_prob.astype(jnp.float32)[..., None] * new_values.reshape(
        requests, key_heads, 1, head_size
    ).astype(jnp.float32)
    return mixture.astype(jnp.bfloat16).reshape(requests, key_heads * sharing * head_size)


def combine_rows(returned_rows, target, gates):
    token_rows, top_count = target.shape
    safe_target = jnp.maximum(target, 0).reshape(-1)
    picked = jnp.take(returned_rows, safe_target, axis=0).reshape(
        token_rows, top_count, returned_rows.shape[1]
    )
    weighting = jnp.where(target >= 0, gates, 0.0)
    return jnp.sum(picked.astype(jnp.float32) * weighting[..., None], axis=1)


def staged(
    queries,
    new_keys,
    new_values,
    cache_keys,
    cache_values,
    lengths,
    out_weight,
    residual,
    norm_gain,
    expert_ids,
    gate_weights,
    w_gate,
    w_up,
    w_down,
):
    attended = attend(queries, new_keys, new_values, cache_keys, cache_values, lengths)
    partial_mix = jnp.dot(
        lax.all_gather(attended, "half", axis=0, tiled=True),
        out_weight,
        preferred_element_type=jnp.float32,
    )
    mixed = lax.psum(partial_mix.astype(jnp.bfloat16), "tp").astype(jnp.float32)
    hidden = residual.astype(jnp.float32) + mixed
    squares = lax.psum(jnp.sum(hidden * hidden, axis=1), "half")
    half_width = hidden.shape[1]
    width = half_width * lax.axis_size("half")
    normed = (hidden * lax.rsqrt(squares / width + EPSILON)[:, None] * norm_gain[None, :]).astype(
        jnp.bfloat16
    )
    token_rows, top_count = expert_ids.shape
    ep_count = lax.axis_size("ep")
    tp_count = lax.axis_size("tp")
    local_experts = w_gate.shape[0]
    capacity = token_rows * top_count * 3 // (2 * EXPERTS)
    slot_count = ep_count * local_experts * capacity
    flat_ids = expert_ids.reshape(-1)
    one_hot = (flat_ids[:, None] == lax.iota(jnp.int32, EXPERTS)[None, :]).astype(jnp.int32)
    earlier = jnp.cumsum(one_hot, axis=0) - one_hot
    slot = jnp.sum(earlier * one_hot, axis=1)
    owner_ep = flat_ids // (local_experts * tp_count)
    owner_tp = flat_ids // local_experts % tp_count
    target = owner_ep * (local_experts * capacity) + flat_ids % local_experts * capacity + slot
    target = jnp.where(owner_tp == lax.axis_index("tp"), target, -1).reshape(token_rows, top_count)
    dispatch_matrix = jnp.any(
        lax.iota(jnp.int32, slot_count)[:, None, None] == target[None, :, :], axis=2
    ).astype(jnp.bfloat16)
    gates = gate_weights / jnp.sum(gate_weights, axis=1, keepdims=True)
    full_rows = lax.all_gather(normed, "half", axis=1, tiled=True)
    outgoing = jnp.dot(dispatch_matrix, full_rows, preferred_element_type=jnp.float32).astype(
        jnp.bfloat16
    )
    arrived = lax.all_to_all(
        outgoing.reshape(ep_count, local_experts, capacity, width),
        "ep",
        split_axis=0,
        concat_axis=0,
        tiled=True,
    )
    gate_part = jnp.einsum("secd,efd->secf", arrived, w_gate, preferred_element_type=jnp.float32)
    up_part = jnp.einsum("secd,efd->secf", arrived, w_up, preferred_element_type=jnp.float32)
    activation = (jax.nn.silu(gate_part) * up_part).astype(jnp.bfloat16)
    expert_out = jnp.einsum(
        "secf,efd->secd", activation, w_down, preferred_element_type=jnp.float32
    ).astype(jnp.bfloat16)
    summed = lax.psum_scatter(
        expert_out.astype(jnp.float32).astype(jnp.bfloat16), "half", scatter_dimension=3, tiled=True
    ).astype(jnp.float32)
    returned = lax.all_to_all(
        summed.reshape(ep_count, local_experts * capacity, half_width).astype(jnp.bfloat16),
        "ep",
        split_axis=0,
        concat_axis=0,
        tiled=True,
    ).astype(jnp.float32)
    term = combine_rows(returned.reshape(slot_count, half_width), target, gates)
    expert_sum = lax.psum_scatter(
        term.astype(jnp.bfloat16), "tp", scatter_dimension=1, tiled=True
    ).astype(jnp.float32)
    slice_width = expert_sum.shape[1]
    own_columns = lax.dynamic_slice_in_dim(
        hidden, lax.axis_index("tp") * slice_width, slice_width, 1
    )
    return (own_columns + expert_sum).astype(jnp.bfloat16)


VMEM_BYTES = 60 * 1024 * 1024
LANES = 128
ROW_TILE = 8
MESH = pl.DeviceIdType.MESH


def remote(src, dst, send, recv, **where):
    return pltpu.make_async_remote_copy(
        src_ref=src,
        dst_ref=dst,
        send_sem=send,
        recv_sem=recv,
        device_id=where,
        device_id_type=MESH,
    )


def partner(index, p):
    bit = 1
    while bit <= p:
        if p & bit:
            index = index + bit - 2 * bit * (index // bit % 2)
        bit *= 2
    return index


def layer_kernel(
    sizes,
    q_ref,
    nk_ref,
    nv_ref,
    len_ref,
    res_ref,
    gain_ref,
    ids_ref,
    gw_ref,
    ck_hbm,
    cv_hbm,
    ow_hbm,
    wg_hbm,
    wu_hbm,
    wd_hbm,
    out_ref,
    ck,
    cv,
    ow,
    wgu,
    wd,
    att_f,
    att,
    gain,
    table,
    mix_out,
    mix_in,
    own_hidden,
    hid,
    xt,
    squares,
    sums,
    act,
    a_out,
    a_in,
    b_out,
    b_in,
    mine,
    c_out,
    c_in,
    load_sem,
    w_sem,
    att_s,
    att_r,
    gain_s,
    gain_r,
    table_s,
    table_r,
    mix_s,
    mix_r,
    hz_s,
    hz_r,
    hx_s,
    hx_r,
    ht_s,
    ht_r,
    a_s,
    a_r,
    b_s,
    b_r,
    c_s,
    c_r,
):
    n_ep, n_half = sizes["ep"], sizes["half"]
    me_z, me_h, me_t = lax.axis_index("ep"), lax.axis_index("half"), lax.axis_index("tp")
    other = 1 - me_t
    requests, context, head_size = ck.shape
    heads = q_ref.shape[1] // head_size
    local, hidden_units = wgu.shape[0], wgu.shape[1] // 2
    block, piece = res_ref.shape[0], res_ref.shape[1] // 2
    rows = n_ep * block
    width = n_half * 2 * piece

    loads = [
        pltpu.make_async_copy(ck_hbm, ck, load_sem.at[0]),
        pltpu.make_async_copy(cv_hbm, cv, load_sem.at[1]),
        pltpu.make_async_copy(ow_hbm, ow, load_sem.at[2]),
    ]
    for load in loads:
        load.start()

    def weight_copy(k, j):
        if k < 2:
            return pltpu.make_async_copy(
                (wg_hbm, wu_hbm)[k].at[j],
                wgu.at[j, pl.ds(k * hidden_units, hidden_units)],
                w_sem.at[k, j],
            )
        part = pl.ds(j * hidden_units, hidden_units)
        return pltpu.make_async_copy(wd_hbm.at[part], wd.at[part], w_sem.at[k, j])

    for j in range(local):
        weight_copy(0, j).start()
        weight_copy(1, j).start()
    for j in range(local):
        weight_copy(2, j).start()

    barrier = pltpu.get_barrier_semaphore()
    pl.semaphore_signal(barrier, inc=1, device_id={"tp": other}, device_id_type=MESH)
    for d in range(1, n_half):
        pl.semaphore_signal(
            barrier, inc=1, device_id={"half": lax.rem(me_h + d, n_half)}, device_id_type=MESH
        )
    for p in range(1, n_ep):
        pl.semaphore_signal(barrier, inc=1, device_id={"ep": partner(me_z, p)}, device_id_type=MESH)

    sent = []

    def go(copy):
        copy.start()
        sent.append(copy)
        return copy

    spread = jnp.broadcast_to(len_ref[...].astype(jnp.float32), (LANES, requests)).T

    loads[0].wait()
    loads[1].wait()
    step = ROW_TILE
    scale = 1.0 / math.sqrt(head_size)
    shape = (heads * step, step * context)
    row = lax.broadcasted_iota(jnp.int32, shape, 0)
    column = lax.broadcasted_iota(jnp.int32, shape, 1)
    same = (row % step) == (column // context)
    position = (column % context).astype(jnp.float32)
    for g in range(requests // step):
        part = pl.ds(g * step, step)
        q_all = q_ref[part].astype(jnp.float32)
        q = jnp.concatenate(
            [q_all[:, h * head_size : (h + 1) * head_size] for h in range(heads)], axis=0
        )
        nk = jnp.concatenate([nk_ref[part].astype(jnp.float32)] * heads, axis=0)
        nv = jnp.concatenate([nv_ref[part].astype(jnp.float32)] * heads, axis=0)
        valid = jnp.concatenate([spread[g * step : (g + 1) * step, :1]] * heads, axis=0)
        keys = ck[part].reshape(step * context, head_size)
        values = cv[part].reshape(step * context, head_size)
        scores = (
            lax.dot_general(
                q.astype(jnp.bfloat16),
                keys,
                (((1,), (1,)), ((), ())),
                preferred_element_type=jnp.float32,
            )
            * scale
        )
        own = jnp.sum(q * nk, axis=1, keepdims=True) * scale
        scores = jnp.where(same & (position < valid), scores, -1e30)
        highest = jnp.maximum(jnp.max(scores, axis=1, keepdims=True), own)
        weights = jnp.exp(scores - highest)
        own_weight = jnp.exp(own - highest)
        inverse = 1.0 / (jnp.sum(weights, axis=1, keepdims=True) + own_weight)
        probs = (weights * inverse).astype(jnp.bfloat16)
        own_prob = (own_weight * inverse).astype(jnp.bfloat16).astype(jnp.float32)
        mixture = jnp.dot(probs, values, preferred_element_type=jnp.float32) + own_prob * nv
        for h in range(heads):
            att_f[part, h * head_size : (h + 1) * head_size] = mixture[h * step : (h + 1) * step]
    att[me_h] = att_f[...].astype(jnp.bfloat16)
    gates = gw_ref[...] / jnp.sum(gw_ref[...], axis=0, keepdims=True)
    expert_row = lax.broadcasted_iota(jnp.int32, (table.shape[1], block), 0)
    own_table = jnp.zeros((table.shape[1], block), jnp.float32)
    for k in range(ids_ref.shape[0]):
        own_table += jnp.where(expert_row == ids_ref[k : k + 1, :], gates[k : k + 1, :], 0.0)
    table[0] = own_table
    gain[me_h] = jnp.broadcast_to(gain_ref[...], gain.shape[1:])

    pl.semaphore_wait(barrier, 1 + (n_half - 1) + (n_ep - 1))
    att_copies = [
        go(
            remote(
                att.at[me_h],
                att.at[me_h],
                att_s.at[d],
                att_r.at[d],
                half=lax.rem(me_h + d, n_half),
            )
        )
        for d in range(1, n_half)
    ]
    gain_copies = [
        go(
            remote(
                gain.at[me_h],
                gain.at[me_h],
                gain_s.at[d],
                gain_r.at[d],
                half=lax.rem(me_h + d, n_half),
            )
        )
        for d in range(1, n_half)
    ]
    table_copies = [
        go(
            remote(
                table.at[0], table.at[p], table_s.at[p], table_r.at[p], ep=partner(me_z, p)
            )
        )
        for p in range(1, n_ep)
    ]
    loads[2].wait()
    for copy in att_copies:
        copy.wait_recv()

    attended = att[...].reshape(block, att.shape[2])
    other_columns = pl.ds(pl.multiple_of(other * piece, piece), piece)
    my_columns = pl.ds(pl.multiple_of(me_t * piece, piece), piece)
    mix_out[...] = jnp.dot(
        attended, ow[:, other_columns], preferred_element_type=jnp.float32
    ).astype(jnp.bfloat16)
    mix_copy = go(remote(mix_out, mix_in, mix_s, mix_r, tp=other))
    mixed = jnp.dot(attended, ow[:, my_columns], preferred_element_type=jnp.float32)
    mixed = mixed + res_ref[:, my_columns].astype(jnp.float32)
    mix_copy.wait_recv()
    hidden = mixed + mix_in[...].astype(jnp.float32)
    own_hidden[...] = hidden
    hid[0, me_h, me_t] = hidden.astype(jnp.bfloat16)

    z_copies = {
        p: go(
            remote(
                hid.at[0, me_h, me_t],
                hid.at[p, me_h, me_t],
                hz_s.at[p],
                hz_r.at[p],
                ep=partner(me_z, p),
            )
        )
        for p in range(1, n_ep)
    }
    x_copies, t_copies = {}, {}

    def take(h, t):
        gain_columns = pl.ds(pl.multiple_of(t * piece, piece), piece)
        scaled = []
        for p in range(n_ep):
            value = hid[p, h, t].astype(jnp.float32)
            square = value * value
            total = square[:, :LANES]
            for k in range(1, piece // LANES):
                total = total + square[:, k * LANES : (k + 1) * LANES]
            squares[p] += total
            scaled.append(value * gain[h, 0:1, gain_columns])
        columns = pl.ds(pl.multiple_of((h * 2 + t) * piece, piece), piece)
        xt[columns, :] = jnp.concatenate(scaled, axis=0).T.astype(jnp.bfloat16)

    def to_sibling(p, dx, h):
        here = hid.at[p, h, me_t]
        t_copies[p, dx] = go(remote(here, here, ht_s.at[dx, p], ht_r.at[dx, p], tp=other))

    def spread_own(group):
        for p in group:
            if p > 0:
                z_copies[p].wait_recv()
            here = hid.at[p, me_h, me_t]
            for dx in range(1, n_half):
                x_copies[p, dx] = go(
                    remote(
                        here,
                        here,
                        hx_s.at[dx, p],
                        hx_r.at[dx, p],
                        half=lax.rem(me_h + dx, n_half),
                    )
                )
            to_sibling(p, 0, me_h)

    def spread_crossed(group):
        for p in group:
            for dx in range(1, n_half):
                x_copies[p, dx].wait_recv()
                to_sibling(p, dx, lax.rem(me_h - dx + n_half, n_half))

    def product(dx, j):
        h = lax.rem(me_h - dx + n_half, n_half)
        span = pl.ds(pl.multiple_of(h * 2 * piece, 2 * piece), 2 * piece)
        return jnp.dot(wgu[j, :, span], xt[span, :], preferred_element_type=jnp.float32)

    def finish(j, inverse):
        weight = jnp.concatenate(
            [table[p, pl.ds((me_z * 2 + me_t) * local + j, 1), :] for p in range(n_ep)], axis=1
        )
        gate = sums[j, :hidden_units] * inverse
        silu = gate / (1.0 + jnp.exp(jnp.minimum(-gate, 88.0)))
        value = silu * (sums[j, hidden_units:] * (inverse * weight))
        act[:, j * hidden_units : (j + 1) * hidden_units] = value.T.astype(jnp.bfloat16)

    a_copies, b_copies, c_copies = {}, {}, {}

    def down(h, t):
        columns = pl.ds(pl.multiple_of((h * 2 + t) * piece, piece), piece)
        return jnp.dot(act[...], wd[:, columns], preferred_element_type=jnp.float32)

    def send_across(dx):
        a_out[dx] = down(lax.rem(me_h + dx, n_half), other).astype(jnp.bfloat16)
        a_copies[dx] = go(remote(a_out.at[dx], a_in.at[dx], a_s.at[dx], a_r.at[dx], tp=other))

    def send_over(dx):
        a_copies[dx].wait_recv()
        total = mine[dx] + a_in[dx].astype(jnp.float32)
        if dx == 0:
            mine[dx] = total
            return
        b_out[dx] = total.astype(jnp.bfloat16)
        for p in reversed(range(n_ep)):
            part = pl.ds(p * block, block)
            b_copies[p, dx] = go(
                remote(
                    b_out.at[dx, part],
                    b_in.at[dx, part],
                    b_s.at[dx, p],
                    b_r.at[dx, p],
                    half=lax.rem(me_h + dx, n_half),
                )
            )

    spread_own(range(n_ep))
    for copy in gain_copies:
        copy.wait_recv()
    squares[...] = jnp.zeros_like(squares)
    take(me_h, me_t)
    for p in range(n_ep):
        t_copies[p, 0].wait_recv()
    take(me_h, other)
    for j in range(local):
        weight_copy(0, j).wait()
        weight_copy(1, j).wait()
        sums[j] = product(0, j)
        if j == local * 3 // 8:
            spread_crossed(range(n_ep // 2))
        if j == local * 3 // 4:
            spread_crossed(range(n_ep // 2, n_ep))
    for dx in range(1, n_half):
        h = lax.rem(me_h - dx + n_half, n_half)
        take(h, me_t)
        for p in range(n_ep):
            t_copies[p, dx].wait_recv()
        take(h, other)
    for copy in table_copies:
        copy.wait_recv()
    total = jnp.sum(squares[...].reshape(rows, LANES).T, axis=0, keepdims=True)
    inverse = lax.rsqrt(total / width + EPSILON)
    for j in range(local):
        for dx in range(1, n_half):
            sums[j] += product(dx, j)
        if j > 0:
            finish(j - 1, inverse)
    finish(local - 1, inverse)
    for j in range(local):
        weight_copy(2, j).wait()
    order = [*range(1, n_half), 0]
    for k, dx in enumerate(order):
        send_across(dx)
        if k > 0:
            send_over(order[k - 1])
        mine[dx] = down(lax.rem(me_h + dx, n_half), me_t)
    send_over(0)
    for p in reversed(range(n_ep)):
        part = slice(p * block, (p + 1) * block)
        total = mine[0, part]
        for dx in range(1, n_half):
            b_copies[p, dx].wait_recv()
            total = total + b_in[dx, part].astype(jnp.float32)
        if p > 0:
            c_out[p] = total.astype(jnp.bfloat16)
            c_copies[p] = go(
                remote(c_out.at[p], c_in.at[p], c_s.at[p], c_r.at[p], ep=partner(me_z, p))
            )
        else:
            own_hidden[...] += total
    result = own_hidden[...]
    for p in range(1, n_ep):
        c_copies[p].wait_recv()
        result = result + c_in[p].astype(jnp.float32)
    out_ref[...] = result.astype(jnp.bfloat16)
    for copy in sent:
        copy.wait_send()


def on_device(sizes, *args):
    (
        queries,
        new_keys,
        new_values,
        cache_keys,
        cache_values,
        lengths,
        out_weight,
        residual,
        norm_gain,
        expert_ids,
        gate_weights,
        w_gate,
        w_up,
        w_down,
    ) = args
    n_ep, n_half, n_tp = sizes["ep"], sizes["half"], sizes["tp"]
    requests, key_heads, context, head_size = cache_keys.shape
    block, half_width = residual.shape
    local, hidden_units, width = w_gate.shape
    piece = half_width // 2
    rows = n_ep * block
    experts = local * n_ep * n_tp
    bf16, f32 = jnp.bfloat16, jnp.float32
    buffers = [
        ((requests, context, head_size), bf16),
        ((requests, context, head_size), bf16),
        (out_weight.shape, bf16),
        ((local, 2 * hidden_units, width), bf16),
        ((local * hidden_units, width), bf16),
        (queries.shape, f32),
        ((n_half,) + queries.shape, bf16),
        ((n_half, ROW_TILE, half_width), f32),
        ((n_ep, experts, block), f32),
        ((block, piece), bf16),
        ((block, piece), bf16),
        ((block, piece), f32),
        ((n_ep, n_half, n_tp, block, piece), bf16),
        ((width, rows), bf16),
        ((n_ep, block, LANES), f32),
        ((local, 2 * hidden_units, rows), f32),
        ((rows, local * hidden_units), bf16),
        ((n_half, rows, piece), bf16),
        ((n_half, rows, piece), bf16),
        ((n_half, rows, piece), bf16),
        ((n_half, rows, piece), bf16),
        ((n_half, rows, piece), f32),
        ((n_ep, block, piece), bf16),
        ((n_ep, block, piece), bf16),
    ]
    held = sum(math.prod(shape) * jnp.dtype(kind).itemsize for shape, kind in buffers)
    fits = (
        held * 9 // 8 < VMEM_BYTES
        and n_tp == 2
        and n_ep > 1
        and n_ep & (n_ep - 1) == 0
        and key_heads == 1
        and hidden_units % LANES == 0
        and piece % LANES == 0
        and requests % (2 * ROW_TILE) == 0
        and block == n_half * requests
    )
    if not fits:
        return staged(*args)
    dma = pltpu.SemaphoreType.DMA
    semaphores = [
        dma((3,)),
        dma((3, local)),
        dma((n_half,)),
        dma((n_half,)),
        dma((n_half,)),
        dma((n_half,)),
        dma((n_ep,)),
        dma((n_ep,)),
        dma,
        dma,
        dma((n_ep,)),
        dma((n_ep,)),
        dma((n_half, n_ep)),
        dma((n_half, n_ep)),
        dma((n_half, n_ep)),
        dma((n_half, n_ep)),
        dma((n_half,)),
        dma((n_half,)),
        dma((n_half, n_ep)),
        dma((n_half, n_ep)),
        dma((n_ep,)),
        dma((n_ep,)),
    ]
    vmem = pl.BlockSpec(memory_space=pltpu.VMEM)
    hbm = pl.BlockSpec(memory_space=pl.ANY)
    return pl.pallas_call(
        functools.partial(layer_kernel, dict(ep=n_ep, half=n_half)),
        out_shape=jax.ShapeDtypeStruct((block, piece), bf16),
        in_specs=[vmem] * 8 + [hbm] * 6,
        out_specs=vmem,
        scratch_shapes=[pltpu.VMEM(shape, kind) for shape, kind in buffers] + semaphores,
        compiler_params=pltpu.CompilerParams(
            collective_id=0, has_side_effects=True, vmem_limit_bytes=VMEM_BYTES
        ),
    )(
        queries,
        new_keys,
        new_values,
        lengths.reshape(1, requests),
        residual,
        norm_gain.reshape(1, half_width),
        expert_ids.T,
        gate_weights.T,
        cache_keys.reshape(requests, context, head_size),
        cache_values.reshape(requests, context, head_size),
        out_weight,
        w_gate,
        w_up,
        w_down.reshape(local * hidden_units, width),
    )


def solution(mesh):
    placed = (
        P(("groups", "ep", "half"), "tp"),
        P(("groups", "ep", "half"), "tp"),
        P(("groups", "ep", "half"), "tp"),
        P(("groups", "ep", "half"), "tp", None, None),
        P(("groups", "ep", "half"), "tp", None, None),
        P(("groups", "ep", "half")),
        P("tp", "half"),
        P(("groups", "ep"), "half"),
        P("half"),
        P(("groups", "ep"), None),
        P(("groups", "ep"), None),
        P(("ep", "tp"), "half", None),
        P(("ep", "tp"), "half", None),
        P(("ep", "tp"), "half", None),
    )
    return jax.shard_map(
        functools.partial(on_device, mesh.shape),
        mesh=mesh,
        in_specs=placed,
        out_specs=P(("groups", "ep"), ("half", "tp")),
        check_vma=False,
    )
```

```python
import functools
import math

import jax
import jax.numpy as jnp
from jax import lax
from jax.experimental import pallas as pl
from jax.experimental.pallas import tpu as pltpu
from jax.sharding import PartitionSpec as P

EXPERTS = 64


EPSILON = 1e-06


def attend(queries, new_keys, new_values, cache_keys, cache_values, lengths):
    requests, key_heads, context, head_size = cache_keys.shape
    sharing = queries.shape[1] // (key_heads * head_size)
    query_blocks = queries.reshape(requests, key_heads, sharing, head_size)
    score_scale = 1.0 / math.sqrt(head_size)
    scores = (
        jnp.einsum("rkgd,rkcd->rkgc", query_blocks, cache_keys, preferred_element_type=jnp.float32)
        * score_scale
    )
    own_score = (
        jnp.einsum(
            "rkgd,rkd->rkg",
            query_blocks,
            new_keys.reshape(requests, key_heads, head_size),
            preferred_element_type=jnp.float32,
        )
        * score_scale
    )
    valid = lax.iota(jnp.int32, context)[None, :] < lengths[:, None]
    scores = jnp.where(valid[:, None, None, :], scores, -1e30)
    highest = jnp.maximum(jnp.max(scores, axis=-1), own_score)
    weights = jnp.exp(scores - highest[..., None])
    own_weight = jnp.exp(own_score - highest)
    denominator = jnp.sum(weights, axis=-1) + own_weight
    probs = (weights / denominator[..., None]).astype(jnp.bfloat16)
    own_prob = (own_weight / denominator).astype(jnp.bfloat16)
    mixture = jnp.einsum("rkgc,rkcd->rkgd", probs, cache_values, preferred_element_type=jnp.float32)
    mixture = mixture + own_prob.astype(jnp.float32)[..., None] * new_values.reshape(
        requests, key_heads, 1, head_size
    ).astype(jnp.float32)
    return mixture.astype(jnp.bfloat16).reshape(requests, key_heads * sharing * head_size)


def combine_rows(returned_rows, target, gates):
    token_rows, top_count = target.shape
    safe_target = jnp.maximum(target, 0).reshape(-1)
    picked = jnp.take(returned_rows, safe_target, axis=0).reshape(
        token_rows, top_count, returned_rows.shape[1]
    )
    weighting = jnp.where(target >= 0, gates, 0.0)
    return jnp.sum(picked.astype(jnp.float32) * weighting[..., None], axis=1)


def staged(
    queries,
    new_keys,
    new_values,
    cache_keys,
    cache_values,
    lengths,
    out_weight,
    residual,
    norm_gain,
    expert_ids,
    gate_weights,
    w_gate,
    w_up,
    w_down,
):
    attended = attend(queries, new_keys, new_values, cache_keys, cache_values, lengths)
    partial_mix = jnp.dot(
        lax.all_gather(attended, "half", axis=0, tiled=True),
        out_weight,
        preferred_element_type=jnp.float32,
    )
    mixed = lax.psum(partial_mix.astype(jnp.bfloat16), "tp").astype(jnp.float32)
    hidden = residual.astype(jnp.float32) + mixed
    squares = lax.psum(jnp.sum(hidden * hidden, axis=1), "half")
    half_width = hidden.shape[1]
    width = half_width * lax.axis_size("half")
    normed = (hidden * lax.rsqrt(squares / width + EPSILON)[:, None] * norm_gain[None, :]).astype(
        jnp.bfloat16
    )
    token_rows, top_count = expert_ids.shape
    ep_count = lax.axis_size("ep")
    tp_count = lax.axis_size("tp")
    local_experts = w_gate.shape[0]
    capacity = token_rows * top_count * 3 // (2 * EXPERTS)
    slot_count = ep_count * local_experts * capacity
    flat_ids = expert_ids.reshape(-1)
    one_hot = (flat_ids[:, None] == lax.iota(jnp.int32, EXPERTS)[None, :]).astype(jnp.int32)
    earlier = jnp.cumsum(one_hot, axis=0) - one_hot
    slot = jnp.sum(earlier * one_hot, axis=1)
    owner_ep = flat_ids // (local_experts * tp_count)
    owner_tp = flat_ids // local_experts % tp_count
    target = owner_ep * (local_experts * capacity) + flat_ids % local_experts * capacity + slot
    target = jnp.where(owner_tp == lax.axis_index("tp"), target, -1).reshape(token_rows, top_count)
    dispatch_matrix = jnp.any(
        lax.iota(jnp.int32, slot_count)[:, None, None] == target[None, :, :], axis=2
    ).astype(jnp.bfloat16)
    gates = gate_weights / jnp.sum(gate_weights, axis=1, keepdims=True)
    full_rows = lax.all_gather(normed, "half", axis=1, tiled=True)
    outgoing = jnp.dot(dispatch_matrix, full_rows, preferred_element_type=jnp.float32).astype(
        jnp.bfloat16
    )
    arrived = lax.all_to_all(
        outgoing.reshape(ep_count, local_experts, capacity, width),
        "ep",
        split_axis=0,
        concat_axis=0,
        tiled=True,
    )
    gate_part = jnp.einsum("secd,efd->secf", arrived, w_gate, preferred_element_type=jnp.float32)
    up_part = jnp.einsum("secd,efd->secf", arrived, w_up, preferred_element_type=jnp.float32)
    activation = (jax.nn.silu(gate_part) * up_part).astype(jnp.bfloat16)
    expert_out = jnp.einsum(
        "secf,efd->secd", activation, w_down, preferred_element_type=jnp.float32
    ).astype(jnp.bfloat16)
    summed = lax.psum_scatter(
        expert_out.astype(jnp.float32).astype(jnp.bfloat16), "half", scatter_dimension=3, tiled=True
    ).astype(jnp.float32)
    returned = lax.all_to_all(
        summed.reshape(ep_count, local_experts * capacity, half_width).astype(jnp.bfloat16),
        "ep",
        split_axis=0,
        concat_axis=0,
        tiled=True,
    ).astype(jnp.float32)
    term = combine_rows(returned.reshape(slot_count, half_width), target, gates)
    expert_sum = lax.psum_scatter(
        term.astype(jnp.bfloat16), "tp", scatter_dimension=1, tiled=True
    ).astype(jnp.float32)
    slice_width = expert_sum.shape[1]
    own_columns = lax.dynamic_slice_in_dim(
        hidden, lax.axis_index("tp") * slice_width, slice_width, 1
    )
    return (own_columns + expert_sum).astype(jnp.bfloat16)


VMEM_BYTES = 60 * 1024 * 1024
LANES = 128
ROW_TILE = 8
MESH = pl.DeviceIdType.MESH


def remote(src, dst, send, recv, **where):
    return pltpu.make_async_remote_copy(
        src_ref=src,
        dst_ref=dst,
        send_sem=send,
        recv_sem=recv,
        device_id=where,
        device_id_type=MESH,
    )


def partner(index, p):
    bit = 1
    while bit <= p:
        if p & bit:
            index = index + bit - 2 * bit * (index // bit % 2)
        bit *= 2
    return index


def each(low, high, body):
    many = 4
    whole = (high - low) // many

    def several(i, carry):
        for k in range(many):
            body(low + i * many + k)
        return carry

    lax.fori_loop(0, whole, several, 0)
    for k in range(low + whole * many, high):
        body(k)


def layer_kernel(
    sizes,
    q_ref,
    nk_ref,
    nv_ref,
    len_ref,
    res_ref,
    gain_ref,
    ids_ref,
    gw_ref,
    ck_hbm,
    cv_hbm,
    ow_hbm,
    wg_hbm,
    wu_hbm,
    wd_hbm,
    out_ref,
    ck,
    cv,
    ow,
    wgu,
    wd,
    att_f,
    att,
    gain,
    table,
    mix_out,
    mix_in,
    own_hidden,
    hid,
    xt,
    squares,
    sums,
    act,
    a_out,
    a_in,
    b_out,
    b_in,
    mine,
    c_out,
    c_in,
    load_sem,
    w_sem,
    att_s,
    att_r,
    gain_s,
    gain_r,
    table_s,
    table_r,
    mix_s,
    mix_r,
    hz_s,
    hz_r,
    hx_s,
    hx_r,
    ht_s,
    ht_r,
    a_s,
    a_r,
    b_s,
    b_r,
    c_s,
    c_r,
):
    n_ep, n_half = sizes["ep"], sizes["half"]
    me_z, me_h, me_t = lax.axis_index("ep"), lax.axis_index("half"), lax.axis_index("tp")
    other = 1 - me_t
    requests, context, head_size = ck.shape
    heads = q_ref.shape[1] // head_size
    local, hidden_units = wgu.shape[0], wgu.shape[1] // 2
    block, piece = res_ref.shape[0], res_ref.shape[1] // 2
    rows = n_ep * block
    width = n_half * 2 * piece

    loads = [
        pltpu.make_async_copy(ck_hbm, ck, load_sem.at[0]),
        pltpu.make_async_copy(cv_hbm, cv, load_sem.at[1]),
        pltpu.make_async_copy(ow_hbm, ow, load_sem.at[2]),
    ]
    for load in loads:
        load.start()

    def weight_copy(k, j):
        if k < 2:
            return pltpu.make_async_copy(
                (wg_hbm, wu_hbm)[k].at[j],
                wgu.at[j, pl.ds(k * hidden_units, hidden_units)],
                w_sem.at[k, j],
            )
        part = pl.ds(j * hidden_units, hidden_units)
        return pltpu.make_async_copy(wd_hbm.at[part], wd.at[part], w_sem.at[k, j])

    def start_weights(kinds, low, high):
        for j in range(low, high):
            for k in kinds:
                weight_copy(k, j).start()

    start_weights((0, 1), 0, local // 2)

    barrier = pltpu.get_barrier_semaphore()
    pl.semaphore_signal(barrier, inc=1, device_id={"tp": other}, device_id_type=MESH)
    for d in range(1, n_half):
        pl.semaphore_signal(
            barrier, inc=1, device_id={"half": lax.rem(me_h + d, n_half)}, device_id_type=MESH
        )
    for p in range(1, n_ep):
        pl.semaphore_signal(barrier, inc=1, device_id={"ep": partner(me_z, p)}, device_id_type=MESH)

    sent = []

    def go(copy):
        copy.start()
        sent.append(copy)
        return copy

    spread = jnp.broadcast_to(len_ref[...].astype(jnp.float32), (LANES, requests)).T

    loads[0].wait()
    loads[1].wait()
    step = ROW_TILE
    scale = 1.0 / math.sqrt(head_size)
    shape = (heads * step, step * context)
    row = lax.broadcasted_iota(jnp.int32, shape, 0)
    column = lax.broadcasted_iota(jnp.int32, shape, 1)
    same = (row % step) == (column // context)
    position = (column % context).astype(jnp.float32)
    for g in range(requests // step):
        part = pl.ds(g * step, step)
        q_all = q_ref[part].astype(jnp.float32)
        q = jnp.concatenate(
            [q_all[:, h * head_size : (h + 1) * head_size] for h in range(heads)], axis=0
        )
        nk = jnp.concatenate([nk_ref[part].astype(jnp.float32)] * heads, axis=0)
        nv = jnp.concatenate([nv_ref[part].astype(jnp.float32)] * heads, axis=0)
        valid = jnp.concatenate([spread[g * step : (g + 1) * step, :1]] * heads, axis=0)
        keys = ck[part].reshape(step * context, head_size)
        values = cv[part].reshape(step * context, head_size)
        scores = (
            lax.dot_general(
                q.astype(jnp.bfloat16),
                keys,
                (((1,), (1,)), ((), ())),
                preferred_element_type=jnp.float32,
            )
            * scale
        )
        own = jnp.sum(q * nk, axis=1, keepdims=True) * scale
        scores = jnp.where(same & (position < valid), scores, -1e30)
        highest = jnp.maximum(jnp.max(scores, axis=1, keepdims=True), own)
        weights = jnp.exp(scores - highest)
        own_weight = jnp.exp(own - highest)
        inverse = 1.0 / (jnp.sum(weights, axis=1, keepdims=True) + own_weight)
        probs = (weights * inverse).astype(jnp.bfloat16)
        own_prob = (own_weight * inverse).astype(jnp.bfloat16).astype(jnp.float32)
        mixture = jnp.dot(probs, values, preferred_element_type=jnp.float32) + own_prob * nv
        for h in range(heads):
            att_f[part, h * head_size : (h + 1) * head_size] = mixture[h * step : (h + 1) * step]
    att[me_h] = att_f[...].astype(jnp.bfloat16)
    gates = gw_ref[...] / jnp.sum(gw_ref[...], axis=0, keepdims=True)
    expert_row = lax.broadcasted_iota(jnp.int32, (table.shape[1], block), 0)
    own_table = jnp.zeros((table.shape[1], block), jnp.float32)
    for k in range(ids_ref.shape[0]):
        own_table += jnp.where(expert_row == ids_ref[k : k + 1, :], gates[k : k + 1, :], 0.0)
    table[0] = own_table
    gain[me_h] = jnp.broadcast_to(gain_ref[...], gain.shape[1:])

    pl.semaphore_wait(barrier, 1 + (n_half - 1) + (n_ep - 1))
    att_copies = [
        go(
            remote(
                att.at[me_h],
                att.at[me_h],
                att_s.at[d],
                att_r.at[d],
                half=lax.rem(me_h + d, n_half),
            )
        )
        for d in range(1, n_half)
    ]
    start_weights((0, 1), local // 2, local)
    gain_copies = [
        go(
            remote(
                gain.at[me_h],
                gain.at[me_h],
                gain_s.at[d],
                gain_r.at[d],
                half=lax.rem(me_h + d, n_half),
            )
        )
        for d in range(1, n_half)
    ]
    table_copies = [
        go(
            remote(
                table.at[0], table.at[p], table_s.at[p], table_r.at[p], ep=partner(me_z, p)
            )
        )
        for p in range(1, n_ep)
    ]
    loads[2].wait()
    for copy in att_copies:
        copy.wait_recv()

    attended = att[...].reshape(block, att.shape[2])
    other_columns = pl.ds(pl.multiple_of(other * piece, piece), piece)
    my_columns = pl.ds(pl.multiple_of(me_t * piece, piece), piece)
    mix_out[...] = jnp.dot(
        attended, ow[:, other_columns], preferred_element_type=jnp.float32
    ).astype(jnp.bfloat16)
    mix_copy = go(remote(mix_out, mix_in, mix_s, mix_r, tp=other))
    mixed = jnp.dot(attended, ow[:, my_columns], preferred_element_type=jnp.float32)
    mixed = mixed + res_ref[:, my_columns].astype(jnp.float32)
    mix_copy.wait_recv()
    hidden = mixed + mix_in[...].astype(jnp.float32)
    own_hidden[...] = hidden
    hid[0, me_h, me_t] = hidden.astype(jnp.bfloat16)

    z_copies = {
        p: go(
            remote(
                hid.at[0, me_h, me_t],
                hid.at[p, me_h, me_t],
                hz_s.at[p],
                hz_r.at[p],
                ep=partner(me_z, p),
            )
        )
        for p in range(1, n_ep)
    }
    start_weights((2,), 0, local)
    x_copies, t_copies = {}, {}

    near, far = range(n_ep // 2), range(n_ep // 2, n_ep)

    def take(group, h, t):
        gain_columns = pl.ds(pl.multiple_of(t * piece, piece), piece)
        scaled = []
        for p in group:
            value = hid[p, h, t].astype(jnp.float32)
            square = value * value
            total = square[:, :LANES]
            for k in range(1, piece // LANES):
                total = total + square[:, k * LANES : (k + 1) * LANES]
            squares[p] += total
            scaled.append(value * gain[h, 0:1, gain_columns])
        columns = pl.ds(pl.multiple_of((h * 2 + t) * piece, piece), piece)
        xt[columns, group[0] * block : (group[-1] + 1) * block] = (
            jnp.concatenate(scaled, axis=0).T.astype(jnp.bfloat16)
        )

    def to_sibling(p, dx, h):
        here = hid.at[p, h, me_t]
        t_copies[p, dx] = go(remote(here, here, ht_s.at[dx, p], ht_r.at[dx, p], tp=other))

    def spread_own(group):
        for p in group:
            if p > 0:
                z_copies[p].wait_recv()
            here = hid.at[p, me_h, me_t]
            for dx in range(1, n_half):
                x_copies[p, dx] = go(
                    remote(
                        here,
                        here,
                        hx_s.at[dx, p],
                        hx_r.at[dx, p],
                        half=lax.rem(me_h + dx, n_half),
                    )
                )
            to_sibling(p, 0, me_h)

    def spread_crossed(group):
        for p in group:
            for dx in range(1, n_half):
                x_copies[p, dx].wait_recv()
                to_sibling(p, dx, lax.rem(me_h - dx + n_half, n_half))

    def product(h, t, j):
        span = pl.ds(pl.multiple_of((h * 2 + t) * piece, piece), piece)
        return jnp.dot(wgu[j, :, span], xt[span, :], preferred_element_type=jnp.float32)

    def finish(h, inverse, j):
        weight = jnp.concatenate(
            [table[p, pl.ds((me_z * 2 + me_t) * local + j, 1), :] for p in range(n_ep)], axis=1
        )
        both = sums[j] + product(h, other, j)
        gate = both[:hidden_units] * inverse
        silu = gate / (1.0 + jnp.exp(jnp.minimum(-gate, 88.0)))
        value = silu * (both[hidden_units:] * (inverse * weight))
        act[:, pl.ds(pl.multiple_of(j * hidden_units, hidden_units), hidden_units)] = value.T.astype(jnp.bfloat16)

    a_copies, b_copies, c_copies = {}, {}, {}

    def down(h, t):
        columns = pl.ds(pl.multiple_of((h * 2 + t) * piece, piece), piece)
        return jnp.dot(act[...], wd[:, columns], preferred_element_type=jnp.float32)

    def send_across(dx):
        a_out[dx] = down(lax.rem(me_h + dx, n_half), other).astype(jnp.bfloat16)
        a_copies[dx] = go(remote(a_out.at[dx], a_in.at[dx], a_s.at[dx], a_r.at[dx], tp=other))

    def send_over(dx):
        a_copies[dx].wait_recv()
        total = mine[dx] + a_in[dx].astype(jnp.float32)
        if dx == 0:
            mine[dx] = total
            return
        b_out[dx - 1] = total.astype(jnp.bfloat16)
        for p in reversed(range(n_ep)):
            part = pl.ds(p * block, block)
            b_copies[p, dx] = go(
                remote(
                    b_out.at[dx - 1, part],
                    b_in.at[dx - 1, part],
                    b_s.at[dx, p],
                    b_r.at[dx, p],
                    half=lax.rem(me_h + dx, n_half),
                )
            )

    spread_own(near)
    for copy in gain_copies:
        copy.wait_recv()
    squares[...] = jnp.zeros_like(squares)
    take(near, me_h, me_t)
    spread_own(far)
    take(far, me_h, me_t)
    def first_piece(j):
        weight_copy(0, j).wait()
        weight_copy(1, j).wait()
        sums[j] = product(me_h, me_t, j)

    def next_piece(h, t, j):
        sums[j] += product(h, t, j)

    each(0, local * 3 // 4, first_piece)
    spread_crossed(near)
    each(local * 3 // 4, local, first_piece)
    for group in (near, far):
        for p in group:
            t_copies[p, 0].wait_recv()
        take(group, me_h, other)
    each(0, local // 2, functools.partial(next_piece, me_h, other))
    spread_crossed(far)
    each(local // 2, local, functools.partial(next_piece, me_h, other))
    for copy in table_copies:
        copy.wait_recv()
    for dx in range(1, n_half):
        h = lax.rem(me_h - dx + n_half, n_half)
        take(near, h, me_t)
        take(far, h, me_t)
        each(0, local, functools.partial(next_piece, h, me_t))
        for group in (near, far):
            for p in group:
                t_copies[p, dx].wait_recv()
            take(group, h, other)
        if dx == n_half - 1:
            total = jnp.sum(squares[...].reshape(rows, LANES).T, axis=0, keepdims=True)
            inverse = lax.rsqrt(total / width + EPSILON)
        if dx < n_half - 1:
            each(0, local, functools.partial(next_piece, h, other))
        else:
            each(0, local, functools.partial(finish, h, inverse))
    for j in range(local):
        weight_copy(2, j).wait()
    order = [*range(1, n_half), 0]
    for dx in order:
        send_across(dx)
        mine[dx] = down(lax.rem(me_h + dx, n_half), me_t)
        send_over(dx)
    for p in reversed(range(n_ep)):
        part = slice(p * block, (p + 1) * block)
        total = mine[0, part]
        for dx in range(1, n_half):
            b_copies[p, dx].wait_recv()
            total = total + b_in[dx - 1, part].astype(jnp.float32)
        if p > 0:
            c_out[p - 1] = total.astype(jnp.bfloat16)
            c_copies[p] = go(
                remote(c_out.at[p - 1], c_in.at[p - 1], c_s.at[p], c_r.at[p], ep=partner(me_z, p))
            )
        else:
            own_hidden[...] += total
    result = own_hidden[...]
    for p in range(1, n_ep):
        c_copies[p].wait_recv()
        result = result + c_in[p - 1].astype(jnp.float32)
    out_ref[...] = result.astype(jnp.bfloat16)
    for copy in sent:
        copy.wait_send()


def on_device(sizes, *args):
    (
        queries,
        new_keys,
        new_values,
        cache_keys,
        cache_values,
        lengths,
        out_weight,
        residual,
        norm_gain,
        expert_ids,
        gate_weights,
        w_gate,
        w_up,
        w_down,
    ) = args
    n_ep, n_half, n_tp = sizes["ep"], sizes["half"], sizes["tp"]
    requests, key_heads, context, head_size = cache_keys.shape
    block, half_width = residual.shape
    local, hidden_units, width = w_gate.shape
    piece = half_width // 2
    rows = n_ep * block
    experts = local * n_ep * n_tp
    bf16, f32 = jnp.bfloat16, jnp.float32
    buffers = [
        ((requests, context, head_size), bf16),
        ((requests, context, head_size), bf16),
        (out_weight.shape, bf16),
        ((local, 2 * hidden_units, width), bf16),
        ((local * hidden_units, width), bf16),
        (queries.shape, f32),
        ((n_half,) + queries.shape, bf16),
        ((n_half, ROW_TILE, half_width), f32),
        ((n_ep, experts, block), f32),
        ((block, piece), bf16),
        ((block, piece), bf16),
        ((block, piece), f32),
        ((n_ep, n_half, n_tp, block, piece), bf16),
        ((width, rows), bf16),
        ((n_ep, block, LANES), f32),
        ((local, 2 * hidden_units, rows), f32),
        ((rows, local * hidden_units), bf16),
        ((n_half, rows, piece), bf16),
        ((n_half, rows, piece), bf16),
        ((n_half - 1, rows, piece), bf16),
        ((n_half - 1, rows, piece), bf16),
        ((n_half, rows, piece), f32),
        ((n_ep - 1, block, piece), bf16),
        ((n_ep - 1, block, piece), bf16),
    ]
    held = sum(math.prod(shape) * jnp.dtype(kind).itemsize for shape, kind in buffers)
    fits = (
        held * 17 // 16 < VMEM_BYTES
        and n_tp == 2
        and n_ep > 1
        and n_ep & (n_ep - 1) == 0
        and key_heads == 1
        and hidden_units % LANES == 0
        and piece % LANES == 0
        and n_half > 1
        and rows % (2 * LANES) == 0
        and requests % (2 * ROW_TILE) == 0
        and block == n_half * requests
    )
    if not fits:
        return staged(*args)
    dma = pltpu.SemaphoreType.DMA
    semaphores = [
        dma((3,)),
        dma((3, local)),
        dma((n_half,)),
        dma((n_half,)),
        dma((n_half,)),
        dma((n_half,)),
        dma((n_ep,)),
        dma((n_ep,)),
        dma,
        dma,
        dma((n_ep,)),
        dma((n_ep,)),
        dma((n_half, n_ep)),
        dma((n_half, n_ep)),
        dma((n_half, n_ep)),
        dma((n_half, n_ep)),
        dma((n_half,)),
        dma((n_half,)),
        dma((n_half, n_ep)),
        dma((n_half, n_ep)),
        dma((n_ep,)),
        dma((n_ep,)),
    ]
    vmem = pl.BlockSpec(memory_space=pltpu.VMEM)
    hbm = pl.BlockSpec(memory_space=pl.ANY)
    return pl.pallas_call(
        functools.partial(layer_kernel, dict(ep=n_ep, half=n_half)),
        out_shape=jax.ShapeDtypeStruct((block, piece), bf16),
        in_specs=[vmem] * 8 + [hbm] * 6,
        out_specs=vmem,
        scratch_shapes=[pltpu.VMEM(shape, kind) for shape, kind in buffers] + semaphores,
        compiler_params=pltpu.CompilerParams(
            collective_id=0, has_side_effects=True, vmem_limit_bytes=VMEM_BYTES
        ),
    )(
        queries,
        new_keys,
        new_values,
        lengths.reshape(1, requests),
        residual,
        norm_gain.reshape(1, half_width),
        expert_ids.T,
        gate_weights.T,
        cache_keys.reshape(requests, context, head_size),
        cache_values.reshape(requests, context, head_size),
        out_weight,
        w_gate,
        w_up,
        w_down.reshape(local * hidden_units, width),
    )


def solution(mesh):
    placed = (
        P(("groups", "ep", "half"), "tp"),
        P(("groups", "ep", "half"), "tp"),
        P(("groups", "ep", "half"), "tp"),
        P(("groups", "ep", "half"), "tp", None, None),
        P(("groups", "ep", "half"), "tp", None, None),
        P(("groups", "ep", "half")),
        P("tp", "half"),
        P(("groups", "ep"), "half"),
        P("half"),
        P(("groups", "ep"), None),
        P(("groups", "ep"), None),
        P(("ep", "tp"), "half", None),
        P(("ep", "tp"), "half", None),
        P(("ep", "tp"), "half", None),
    )
    return jax.shard_map(
        functools.partial(on_device, mesh.shape),
        mesh=mesh,
        in_specs=placed,
        out_specs=P(("groups", "ep"), ("half", "tp")),
        check_vma=False,
    )
```

```python
import functools
import math

import jax
import jax.numpy as jnp
from jax import lax
from jax.experimental import pallas as pl
from jax.experimental.pallas import tpu as pltpu
from jax.sharding import PartitionSpec as P

EXPERTS = 64


EPSILON = 1e-06


def attend(queries, new_keys, new_values, cache_keys, cache_values, lengths):
    requests, key_heads, context, head_size = cache_keys.shape
    sharing = queries.shape[1] // (key_heads * head_size)
    query_blocks = queries.reshape(requests, key_heads, sharing, head_size)
    score_scale = 1.0 / math.sqrt(head_size)
    scores = (
        jnp.einsum("rkgd,rkcd->rkgc", query_blocks, cache_keys, preferred_element_type=jnp.float32)
        * score_scale
    )
    own_score = (
        jnp.einsum(
            "rkgd,rkd->rkg",
            query_blocks,
            new_keys.reshape(requests, key_heads, head_size),
            preferred_element_type=jnp.float32,
        )
        * score_scale
    )
    valid = lax.iota(jnp.int32, context)[None, :] < lengths[:, None]
    scores = jnp.where(valid[:, None, None, :], scores, -1e30)
    highest = jnp.maximum(jnp.max(scores, axis=-1), own_score)
    weights = jnp.exp(scores - highest[..., None])
    own_weight = jnp.exp(own_score - highest)
    denominator = jnp.sum(weights, axis=-1) + own_weight
    probs = (weights / denominator[..., None]).astype(jnp.bfloat16)
    own_prob = (own_weight / denominator).astype(jnp.bfloat16)
    mixture = jnp.einsum("rkgc,rkcd->rkgd", probs, cache_values, preferred_element_type=jnp.float32)
    mixture = mixture + own_prob.astype(jnp.float32)[..., None] * new_values.reshape(
        requests, key_heads, 1, head_size
    ).astype(jnp.float32)
    return mixture.astype(jnp.bfloat16).reshape(requests, key_heads * sharing * head_size)


def combine_rows(returned_rows, target, gates):
    token_rows, top_count = target.shape
    safe_target = jnp.maximum(target, 0).reshape(-1)
    picked = jnp.take(returned_rows, safe_target, axis=0).reshape(
        token_rows, top_count, returned_rows.shape[1]
    )
    weighting = jnp.where(target >= 0, gates, 0.0)
    return jnp.sum(picked.astype(jnp.float32) * weighting[..., None], axis=1)


def staged(
    queries,
    new_keys,
    new_values,
    cache_keys,
    cache_values,
    lengths,
    out_weight,
    residual,
    norm_gain,
    expert_ids,
    gate_weights,
    w_gate,
    w_up,
    w_down,
):
    attended = attend(queries, new_keys, new_values, cache_keys, cache_values, lengths)
    partial_mix = jnp.dot(
        lax.all_gather(attended, "half", axis=0, tiled=True),
        out_weight,
        preferred_element_type=jnp.float32,
    )
    mixed = lax.psum(partial_mix.astype(jnp.bfloat16), "tp").astype(jnp.float32)
    hidden = residual.astype(jnp.float32) + mixed
    squares = lax.psum(jnp.sum(hidden * hidden, axis=1), "half")
    half_width = hidden.shape[1]
    width = half_width * lax.axis_size("half")
    normed = (hidden * lax.rsqrt(squares / width + EPSILON)[:, None] * norm_gain[None, :]).astype(
        jnp.bfloat16
    )
    token_rows, top_count = expert_ids.shape
    ep_count = lax.axis_size("ep")
    tp_count = lax.axis_size("tp")
    local_experts = w_gate.shape[0]
    capacity = token_rows * top_count * 3 // (2 * EXPERTS)
    slot_count = ep_count * local_experts * capacity
    flat_ids = expert_ids.reshape(-1)
    one_hot = (flat_ids[:, None] == lax.iota(jnp.int32, EXPERTS)[None, :]).astype(jnp.int32)
    earlier = jnp.cumsum(one_hot, axis=0) - one_hot
    slot = jnp.sum(earlier * one_hot, axis=1)
    owner_ep = flat_ids // (local_experts * tp_count)
    owner_tp = flat_ids // local_experts % tp_count
    target = owner_ep * (local_experts * capacity) + flat_ids % local_experts * capacity + slot
    target = jnp.where(owner_tp == lax.axis_index("tp"), target, -1).reshape(token_rows, top_count)
    dispatch_matrix = jnp.any(
        lax.iota(jnp.int32, slot_count)[:, None, None] == target[None, :, :], axis=2
    ).astype(jnp.bfloat16)
    gates = gate_weights / jnp.sum(gate_weights, axis=1, keepdims=True)
    full_rows = lax.all_gather(normed, "half", axis=1, tiled=True)
    outgoing = jnp.dot(dispatch_matrix, full_rows, preferred_element_type=jnp.float32).astype(
        jnp.bfloat16
    )
    arrived = lax.all_to_all(
        outgoing.reshape(ep_count, local_experts, capacity, width),
        "ep",
        split_axis=0,
        concat_axis=0,
        tiled=True,
    )
    gate_part = jnp.einsum("secd,efd->secf", arrived, w_gate, preferred_element_type=jnp.float32)
    up_part = jnp.einsum("secd,efd->secf", arrived, w_up, preferred_element_type=jnp.float32)
    activation = (jax.nn.silu(gate_part) * up_part).astype(jnp.bfloat16)
    expert_out = jnp.einsum(
        "secf,efd->secd", activation, w_down, preferred_element_type=jnp.float32
    ).astype(jnp.bfloat16)
    summed = lax.psum_scatter(
        expert_out.astype(jnp.float32).astype(jnp.bfloat16), "half", scatter_dimension=3, tiled=True
    ).astype(jnp.float32)
    returned = lax.all_to_all(
        summed.reshape(ep_count, local_experts * capacity, half_width).astype(jnp.bfloat16),
        "ep",
        split_axis=0,
        concat_axis=0,
        tiled=True,
    ).astype(jnp.float32)
    term = combine_rows(returned.reshape(slot_count, half_width), target, gates)
    expert_sum = lax.psum_scatter(
        term.astype(jnp.bfloat16), "tp", scatter_dimension=1, tiled=True
    ).astype(jnp.float32)
    slice_width = expert_sum.shape[1]
    own_columns = lax.dynamic_slice_in_dim(
        hidden, lax.axis_index("tp") * slice_width, slice_width, 1
    )
    return (own_columns + expert_sum).astype(jnp.bfloat16)


VMEM_BYTES = 60 * 1024 * 1024
LANES = 128
ROW_TILE = 8
MESH = pl.DeviceIdType.MESH


def remote(src, dst, send, recv, **where):
    return pltpu.make_async_remote_copy(
        src_ref=src,
        dst_ref=dst,
        send_sem=send,
        recv_sem=recv,
        device_id=where,
        device_id_type=MESH,
    )


def partner(index, p):
    bit = 1
    while bit <= p:
        if p & bit:
            index = index + bit - 2 * bit * (index // bit % 2)
        bit *= 2
    return index


def each(low, high, body):
    many = 4
    whole = (high - low) // many

    def several(i, carry):
        for k in range(many):
            body(low + i * many + k)
        return carry

    lax.fori_loop(0, whole, several, 0)
    for k in range(low + whole * many, high):
        body(k)


def layer_kernel(
    sizes,
    q_ref,
    nk_ref,
    nv_ref,
    len_ref,
    res_ref,
    gain_ref,
    ids_ref,
    gw_ref,
    ck_hbm,
    cv_hbm,
    ow_hbm,
    wg_hbm,
    wu_hbm,
    wd_hbm,
    out_ref,
    ck,
    cv,
    ow,
    wgu,
    wd,
    att_f,
    att,
    gain,
    table,
    mix_out,
    mix_in,
    own_hidden,
    hid,
    xt,
    squares,
    sums,
    act,
    a_out,
    a_in,
    b_out,
    b_in,
    mine,
    c_out,
    c_in,
    load_sem,
    w_sem,
    att_s,
    att_r,
    gain_s,
    gain_r,
    table_s,
    table_r,
    mix_s,
    mix_r,
    hz_s,
    hz_r,
    hx_s,
    hx_r,
    ht_s,
    ht_r,
    a_s,
    a_r,
    b_s,
    b_r,
    c_s,
    c_r,
):
    n_ep, n_half = sizes["ep"], sizes["half"]
    me_z, me_h, me_t = lax.axis_index("ep"), lax.axis_index("half"), lax.axis_index("tp")
    other = 1 - me_t
    requests, context, head_size = ck.shape
    heads = q_ref.shape[1] // head_size
    local, hidden_units = wgu.shape[0], wgu.shape[1] // 2
    block, piece = res_ref.shape[0], res_ref.shape[1] // 2
    rows = n_ep * block
    width = n_half * 2 * piece

    loads = [
        pltpu.make_async_copy(ck_hbm, ck, load_sem.at[0]),
        pltpu.make_async_copy(cv_hbm, cv, load_sem.at[1]),
        pltpu.make_async_copy(ow_hbm, ow, load_sem.at[2]),
    ]
    for load in loads:
        load.start()

    def weight_copy(k, j):
        if k < 2:
            return pltpu.make_async_copy(
                (wg_hbm, wu_hbm)[k].at[j],
                wgu.at[j, pl.ds(k * hidden_units, hidden_units)],
                w_sem.at[k, j],
            )
        part = pl.ds(j * hidden_units, hidden_units)
        return pltpu.make_async_copy(wd_hbm.at[part], wd.at[part], w_sem.at[k, j])

    def start_weights(kinds, low, high):
        for j in range(low, high):
            for k in kinds:
                weight_copy(k, j).start()

    start_weights((0, 1), 0, local // 2)

    barrier = pltpu.get_barrier_semaphore()
    pl.semaphore_signal(barrier, inc=1, device_id={"tp": other}, device_id_type=MESH)
    for d in range(1, n_half):
        pl.semaphore_signal(
            barrier, inc=1, device_id={"half": lax.rem(me_h + d, n_half)}, device_id_type=MESH
        )
    for p in range(1, n_ep):
        pl.semaphore_signal(barrier, inc=1, device_id={"ep": partner(me_z, p)}, device_id_type=MESH)

    sent = []

    def go(copy):
        copy.start()
        sent.append(copy)
        return copy

    spread = jnp.broadcast_to(len_ref[...].astype(jnp.float32), (LANES, requests)).T

    loads[0].wait()
    loads[1].wait()
    step = ROW_TILE
    scale = 1.0 / math.sqrt(head_size)
    shape = (heads * step, step * context)
    row = lax.broadcasted_iota(jnp.int32, shape, 0)
    column = lax.broadcasted_iota(jnp.int32, shape, 1)
    same = (row % step) == (column // context)
    position = (column % context).astype(jnp.float32)
    for g in range(requests // step):
        part = pl.ds(g * step, step)
        q_all = q_ref[part].astype(jnp.float32)
        q = jnp.concatenate(
            [q_all[:, h * head_size : (h + 1) * head_size] for h in range(heads)], axis=0
        )
        nk = jnp.concatenate([nk_ref[part].astype(jnp.float32)] * heads, axis=0)
        nv = jnp.concatenate([nv_ref[part].astype(jnp.float32)] * heads, axis=0)
        valid = jnp.concatenate([spread[g * step : (g + 1) * step, :1]] * heads, axis=0)
        keys = ck[part].reshape(step * context, head_size)
        values = cv[part].reshape(step * context, head_size)
        scores = (
            lax.dot_general(
                q.astype(jnp.bfloat16),
                keys,
                (((1,), (1,)), ((), ())),
                preferred_element_type=jnp.float32,
            )
            * scale
        )
        own = jnp.sum(q * nk, axis=1, keepdims=True) * scale
        scores = jnp.where(same & (position < valid), scores, -1e30)
        highest = jnp.maximum(jnp.max(scores, axis=1, keepdims=True), own)
        weights = jnp.exp(scores - highest)
        own_weight = jnp.exp(own - highest)
        inverse = 1.0 / (jnp.sum(weights, axis=1, keepdims=True) + own_weight)
        probs = (weights * inverse).astype(jnp.bfloat16)
        own_prob = (own_weight * inverse).astype(jnp.bfloat16).astype(jnp.float32)
        mixture = jnp.dot(probs, values, preferred_element_type=jnp.float32) + own_prob * nv
        for h in range(heads):
            att_f[part, h * head_size : (h + 1) * head_size] = mixture[h * step : (h + 1) * step]
    att[me_h] = att_f[...].astype(jnp.bfloat16)
    gates = gw_ref[...] / jnp.sum(gw_ref[...], axis=0, keepdims=True)
    expert_row = lax.broadcasted_iota(jnp.int32, (table.shape[1], block), 0)
    own_table = jnp.zeros((table.shape[1], block), jnp.float32)
    for k in range(ids_ref.shape[0]):
        own_table += jnp.where(expert_row == ids_ref[k : k + 1, :], gates[k : k + 1, :], 0.0)
    table[0] = own_table
    gain[me_h] = jnp.broadcast_to(gain_ref[...], gain.shape[1:])

    pl.semaphore_wait(barrier, 1 + (n_half - 1) + (n_ep - 1))
    att_copies = [
        go(
            remote(
                att.at[me_h],
                att.at[me_h],
                att_s.at[d],
                att_r.at[d],
                half=lax.rem(me_h + d, n_half),
            )
        )
        for d in range(1, n_half)
    ]
    start_weights((0, 1), local // 2, local * 3 // 4)
    gain_copies = [
        go(
            remote(
                gain.at[me_h],
                gain.at[me_h],
                gain_s.at[d],
                gain_r.at[d],
                half=lax.rem(me_h + d, n_half),
            )
        )
        for d in range(1, n_half)
    ]
    table_copies = [
        go(
            remote(
                table.at[0], table.at[p], table_s.at[p], table_r.at[p], ep=partner(me_z, p)
            )
        )
        for p in range(1, n_ep)
    ]
    loads[2].wait()
    for copy in att_copies:
        copy.wait_recv()

    attended = att[...].reshape(block, att.shape[2])
    other_columns = pl.ds(pl.multiple_of(other * piece, piece), piece)
    my_columns = pl.ds(pl.multiple_of(me_t * piece, piece), piece)
    mix_out[...] = jnp.dot(
        attended, ow[:, other_columns], preferred_element_type=jnp.float32
    ).astype(jnp.bfloat16)
    mix_copy = go(remote(mix_out, mix_in, mix_s, mix_r, tp=other))
    start_weights((0, 1), local * 3 // 4, local)
    mixed = jnp.dot(attended, ow[:, my_columns], preferred_element_type=jnp.float32)
    mixed = mixed + res_ref[:, my_columns].astype(jnp.float32)
    mix_copy.wait_recv()
    hidden = mixed + mix_in[...].astype(jnp.float32)
    own_hidden[...] = hidden
    hid[0, me_h, me_t] = hidden.astype(jnp.bfloat16)

    z_copies = {
        p: go(
            remote(
                hid.at[0, me_h, me_t],
                hid.at[p, me_h, me_t],
                hz_s.at[p],
                hz_r.at[p],
                ep=partner(me_z, p),
            )
        )
        for p in range(1, n_ep)
    }
    x_copies, t_copies = {}, {}

    near, far = range(n_ep // 2), range(n_ep // 2, n_ep)

    def take(group, h, t):
        gain_columns = pl.ds(pl.multiple_of(t * piece, piece), piece)
        scaled = []
        for p in group:
            value = hid[p, h, t].astype(jnp.float32)
            square = value * value
            total = square[:, :LANES]
            for k in range(1, piece // LANES):
                total = total + square[:, k * LANES : (k + 1) * LANES]
            squares[p] += total
            scaled.append(value * gain[h, 0:1, gain_columns])
        columns = pl.ds(pl.multiple_of((h * 2 + t) * piece, piece), piece)
        xt[columns, group[0] * block : (group[-1] + 1) * block] = (
            jnp.concatenate(scaled, axis=0).T.astype(jnp.bfloat16)
        )

    def to_sibling(p, dx, h):
        here = hid.at[p, h, me_t]
        t_copies[p, dx] = go(remote(here, here, ht_s.at[dx, p], ht_r.at[dx, p], tp=other))

    def spread_own(group):
        for p in group:
            if p > 0:
                z_copies[p].wait_recv()
            here = hid.at[p, me_h, me_t]
            for dx in range(1, n_half):
                x_copies[p, dx] = go(
                    remote(
                        here,
                        here,
                        hx_s.at[dx, p],
                        hx_r.at[dx, p],
                        half=lax.rem(me_h + dx, n_half),
                    )
                )
            to_sibling(p, 0, me_h)

    def spread_crossed(group):
        for p in group:
            for dx in range(1, n_half):
                x_copies[p, dx].wait_recv()
                to_sibling(p, dx, lax.rem(me_h - dx + n_half, n_half))

    def product(h, t, j):
        span = pl.ds(pl.multiple_of((h * 2 + t) * piece, piece), piece)
        return jnp.dot(wgu[j, :, span], xt[span, :], preferred_element_type=jnp.float32)

    def finish(h, inverse, j):
        weight = jnp.concatenate(
            [table[p, pl.ds((me_z * 2 + me_t) * local + j, 1), :] for p in range(n_ep)], axis=1
        )
        both = sums[j] + product(h, other, j)
        gate = both[:hidden_units] * inverse
        silu = gate / (1.0 + jnp.exp(jnp.minimum(-gate, 88.0)))
        value = silu * (both[hidden_units:] * (inverse * weight))
        act[:, pl.ds(pl.multiple_of(j * hidden_units, hidden_units), hidden_units)] = value.T.astype(jnp.bfloat16)

    a_copies, b_copies, c_copies = {}, {}, {}

    def down(h, t):
        columns = pl.ds(pl.multiple_of((h * 2 + t) * piece, piece), piece)
        return jnp.dot(act[...], wd[:, columns], preferred_element_type=jnp.float32)

    def send_across(dx):
        a_out[dx] = down(lax.rem(me_h + dx, n_half), other).astype(jnp.bfloat16)
        a_copies[dx] = go(remote(a_out.at[dx], a_in.at[dx], a_s.at[dx], a_r.at[dx], tp=other))

    def send_over(dx):
        a_copies[dx].wait_recv()
        total = mine[dx] + a_in[dx].astype(jnp.float32)
        if dx == 0:
            mine[dx] = total
            return
        for p in reversed(range(n_ep)):
            part = pl.ds(p * block, block)
            b_out[dx - 1, part] = total[p * block : (p + 1) * block].astype(jnp.bfloat16)
            b_copies[p, dx] = go(
                remote(
                    b_out.at[dx - 1, part],
                    b_in.at[dx - 1, part],
                    b_s.at[dx, p],
                    b_r.at[dx, p],
                    half=lax.rem(me_h + dx, n_half),
                )
            )

    spread_own(near)
    for copy in gain_copies:
        copy.wait_recv()
    squares[...] = jnp.zeros_like(squares)
    take(near, me_h, me_t)
    spread_own(far)
    take(far, me_h, me_t)
    def first_piece(j):
        weight_copy(0, j).wait()
        weight_copy(1, j).wait()
        weight_copy(2, j).start()
        sums[j] = product(me_h, me_t, j)

    def next_piece(h, t, j):
        sums[j] += product(h, t, j)

    each(0, local // 2, first_piece)
    spread_crossed(near)
    each(local // 2, local, first_piece)
    for group in (near, far):
        for p in group:
            t_copies[p, 0].wait_recv()
        take(group, me_h, other)
    each(0, local // 2, functools.partial(next_piece, me_h, other))
    spread_crossed(far)
    each(local // 2, local, functools.partial(next_piece, me_h, other))
    for copy in table_copies:
        copy.wait_recv()
    for dx in range(1, n_half):
        h = lax.rem(me_h - dx + n_half, n_half)
        take(near, h, me_t)
        take(far, h, me_t)
        each(0, local, functools.partial(next_piece, h, me_t))
        for group in (near, far):
            for p in group:
                t_copies[p, dx].wait_recv()
            take(group, h, other)
        if dx == n_half - 1:
            total = jnp.sum(squares[...].reshape(rows, LANES).T, axis=0, keepdims=True)
            inverse = lax.rsqrt(total / width + EPSILON)
        if dx < n_half - 1:
            each(0, local, functools.partial(next_piece, h, other))
        else:
            each(0, local, functools.partial(finish, h, inverse))
    for j in range(local):
        weight_copy(2, j).wait()
    order = [*range(1, n_half), 0]
    for dx in order:
        send_across(dx)
        mine[dx] = down(lax.rem(me_h + dx, n_half), me_t)
        send_over(dx)
    for p in reversed(range(n_ep)):
        part = slice(p * block, (p + 1) * block)
        total = mine[0, part]
        for dx in range(1, n_half):
            b_copies[p, dx].wait_recv()
            total = total + b_in[dx - 1, part].astype(jnp.float32)
        if p > 0:
            c_out[p - 1] = total.astype(jnp.bfloat16)
            c_copies[p] = go(
                remote(c_out.at[p - 1], c_in.at[p - 1], c_s.at[p], c_r.at[p], ep=partner(me_z, p))
            )
        else:
            own_hidden[...] += total
    result = own_hidden[...]
    for p in range(1, n_ep):
        c_copies[p].wait_recv()
        result = result + c_in[p - 1].astype(jnp.float32)
    out_ref[...] = result.astype(jnp.bfloat16)
    for copy in sent:
        copy.wait_send()


def on_device(sizes, *args):
    (
        queries,
        new_keys,
        new_values,
        cache_keys,
        cache_values,
        lengths,
        out_weight,
        residual,
        norm_gain,
        expert_ids,
        gate_weights,
        w_gate,
        w_up,
        w_down,
    ) = args
    n_ep, n_half, n_tp = sizes["ep"], sizes["half"], sizes["tp"]
    requests, key_heads, context, head_size = cache_keys.shape
    block, half_width = residual.shape
    local, hidden_units, width = w_gate.shape
    piece = half_width // 2
    rows = n_ep * block
    experts = local * n_ep * n_tp
    bf16, f32 = jnp.bfloat16, jnp.float32
    buffers = [
        ((requests, context, head_size), bf16),
        ((requests, context, head_size), bf16),
        (out_weight.shape, bf16),
        ((local, 2 * hidden_units, width), bf16),
        ((local * hidden_units, width), bf16),
        (queries.shape, f32),
        ((n_half,) + queries.shape, bf16),
        ((n_half, ROW_TILE, half_width), f32),
        ((n_ep, experts, block), f32),
        ((block, piece), bf16),
        ((block, piece), bf16),
        ((block, piece), f32),
        ((n_ep, n_half, n_tp, block, piece), bf16),
        ((width, rows), bf16),
        ((n_ep, block, LANES), f32),
        ((local, 2 * hidden_units, rows), f32),
        ((rows, local * hidden_units), bf16),
        ((n_half, rows, piece), bf16),
        ((n_half, rows, piece), bf16),
        ((n_half - 1, rows, piece), bf16),
        ((n_half - 1, rows, piece), bf16),
        ((n_half, rows, piece), f32),
        ((n_ep - 1, block, piece), bf16),
        ((n_ep - 1, block, piece), bf16),
    ]
    held = sum(math.prod(shape) * jnp.dtype(kind).itemsize for shape, kind in buffers)
    fits = (
        held * 17 // 16 < VMEM_BYTES
        and n_tp == 2
        and n_ep > 1
        and n_ep & (n_ep - 1) == 0
        and key_heads == 1
        and hidden_units % LANES == 0
        and piece % LANES == 0
        and n_half > 1
        and rows % (2 * LANES) == 0
        and requests % (2 * ROW_TILE) == 0
        and block == n_half * requests
    )
    if not fits:
        return staged(*args)
    dma = pltpu.SemaphoreType.DMA
    semaphores = [
        dma((3,)),
        dma((3, local)),
        dma((n_half,)),
        dma((n_half,)),
        dma((n_half,)),
        dma((n_half,)),
        dma((n_ep,)),
        dma((n_ep,)),
        dma,
        dma,
        dma((n_ep,)),
        dma((n_ep,)),
        dma((n_half, n_ep)),
        dma((n_half, n_ep)),
        dma((n_half, n_ep)),
        dma((n_half, n_ep)),
        dma((n_half,)),
        dma((n_half,)),
        dma((n_half, n_ep)),
        dma((n_half, n_ep)),
        dma((n_ep,)),
        dma((n_ep,)),
    ]
    vmem = pl.BlockSpec(memory_space=pltpu.VMEM)
    hbm = pl.BlockSpec(memory_space=pl.ANY)
    return pl.pallas_call(
        functools.partial(layer_kernel, dict(ep=n_ep, half=n_half)),
        out_shape=jax.ShapeDtypeStruct((block, piece), bf16),
        in_specs=[vmem] * 8 + [hbm] * 6,
        out_specs=vmem,
        scratch_shapes=[pltpu.VMEM(shape, kind) for shape, kind in buffers] + semaphores,
        compiler_params=pltpu.CompilerParams(
            collective_id=0, has_side_effects=True, vmem_limit_bytes=VMEM_BYTES
        ),
    )(
        queries,
        new_keys,
        new_values,
        lengths.reshape(1, requests),
        residual,
        norm_gain.reshape(1, half_width),
        expert_ids.T,
        gate_weights.T,
        cache_keys.reshape(requests, context, head_size),
        cache_values.reshape(requests, context, head_size),
        out_weight,
        w_gate,
        w_up,
        w_down.reshape(local * hidden_units, width),
    )


def solution(mesh):
    placed = (
        P(("groups", "ep", "half"), "tp"),
        P(("groups", "ep", "half"), "tp"),
        P(("groups", "ep", "half"), "tp"),
        P(("groups", "ep", "half"), "tp", None, None),
        P(("groups", "ep", "half"), "tp", None, None),
        P(("groups", "ep", "half")),
        P("tp", "half"),
        P(("groups", "ep"), "half"),
        P("half"),
        P(("groups", "ep"), None),
        P(("groups", "ep"), None),
        P(("ep", "tp"), "half", None),
        P(("ep", "tp"), "half", None),
        P(("ep", "tp"), "half", None),
    )
    return jax.shard_map(
        functools.partial(on_device, mesh.shape),
        mesh=mesh,
        in_specs=placed,
        out_specs=P(("groups", "ep"), ("half", "tp")),
        check_vma=False,
    )
```

```python
import functools
import math

import jax
import jax.numpy as jnp
from jax import lax
from jax.experimental import pallas as pl
from jax.experimental.pallas import tpu as pltpu
from jax.sharding import PartitionSpec as P

EXPERTS = 64


EPSILON = 1e-06


def attend(queries, new_keys, new_values, cache_keys, cache_values, lengths):
    requests, key_heads, context, head_size = cache_keys.shape
    sharing = queries.shape[1] // (key_heads * head_size)
    query_blocks = queries.reshape(requests, key_heads, sharing, head_size)
    score_scale = 1.0 / math.sqrt(head_size)
    scores = (
        jnp.einsum("rkgd,rkcd->rkgc", query_blocks, cache_keys, preferred_element_type=jnp.float32)
        * score_scale
    )
    own_score = (
        jnp.einsum(
            "rkgd,rkd->rkg",
            query_blocks,
            new_keys.reshape(requests, key_heads, head_size),
            preferred_element_type=jnp.float32,
        )
        * score_scale
    )
    valid = lax.iota(jnp.int32, context)[None, :] < lengths[:, None]
    scores = jnp.where(valid[:, None, None, :], scores, -1e30)
    highest = jnp.maximum(jnp.max(scores, axis=-1), own_score)
    weights = jnp.exp(scores - highest[..., None])
    own_weight = jnp.exp(own_score - highest)
    denominator = jnp.sum(weights, axis=-1) + own_weight
    probs = (weights / denominator[..., None]).astype(jnp.bfloat16)
    own_prob = (own_weight / denominator).astype(jnp.bfloat16)
    mixture = jnp.einsum("rkgc,rkcd->rkgd", probs, cache_values, preferred_element_type=jnp.float32)
    mixture = mixture + own_prob.astype(jnp.float32)[..., None] * new_values.reshape(
        requests, key_heads, 1, head_size
    ).astype(jnp.float32)
    return mixture.astype(jnp.bfloat16).reshape(requests, key_heads * sharing * head_size)


def combine_rows(returned_rows, target, gates):
    token_rows, top_count = target.shape
    safe_target = jnp.maximum(target, 0).reshape(-1)
    picked = jnp.take(returned_rows, safe_target, axis=0).reshape(
        token_rows, top_count, returned_rows.shape[1]
    )
    weighting = jnp.where(target >= 0, gates, 0.0)
    return jnp.sum(picked.astype(jnp.float32) * weighting[..., None], axis=1)


def staged(
    queries,
    new_keys,
    new_values,
    cache_keys,
    cache_values,
    lengths,
    out_weight,
    residual,
    norm_gain,
    expert_ids,
    gate_weights,
    w_gate,
    w_up,
    w_down,
):
    attended = attend(queries, new_keys, new_values, cache_keys, cache_values, lengths)
    partial_mix = jnp.dot(
        lax.all_gather(attended, "half", axis=0, tiled=True),
        out_weight,
        preferred_element_type=jnp.float32,
    )
    mixed = lax.psum(partial_mix.astype(jnp.bfloat16), "tp").astype(jnp.float32)
    hidden = residual.astype(jnp.float32) + mixed
    squares = lax.psum(jnp.sum(hidden * hidden, axis=1), "half")
    half_width = hidden.shape[1]
    width = half_width * lax.axis_size("half")
    normed = (hidden * lax.rsqrt(squares / width + EPSILON)[:, None] * norm_gain[None, :]).astype(
        jnp.bfloat16
    )
    token_rows, top_count = expert_ids.shape
    ep_count = lax.axis_size("ep")
    tp_count = lax.axis_size("tp")
    local_experts = w_gate.shape[0]
    capacity = token_rows * top_count * 3 // (2 * EXPERTS)
    slot_count = ep_count * local_experts * capacity
    flat_ids = expert_ids.reshape(-1)
    one_hot = (flat_ids[:, None] == lax.iota(jnp.int32, EXPERTS)[None, :]).astype(jnp.int32)
    earlier = jnp.cumsum(one_hot, axis=0) - one_hot
    slot = jnp.sum(earlier * one_hot, axis=1)
    owner_ep = flat_ids // (local_experts * tp_count)
    owner_tp = flat_ids // local_experts % tp_count
    target = owner_ep * (local_experts * capacity) + flat_ids % local_experts * capacity + slot
    target = jnp.where(owner_tp == lax.axis_index("tp"), target, -1).reshape(token_rows, top_count)
    dispatch_matrix = jnp.any(
        lax.iota(jnp.int32, slot_count)[:, None, None] == target[None, :, :], axis=2
    ).astype(jnp.bfloat16)
    gates = gate_weights / jnp.sum(gate_weights, axis=1, keepdims=True)
    full_rows = lax.all_gather(normed, "half", axis=1, tiled=True)
    outgoing = jnp.dot(dispatch_matrix, full_rows, preferred_element_type=jnp.float32).astype(
        jnp.bfloat16
    )
    arrived = lax.all_to_all(
        outgoing.reshape(ep_count, local_experts, capacity, width),
        "ep",
        split_axis=0,
        concat_axis=0,
        tiled=True,
    )
    gate_part = jnp.einsum("secd,efd->secf", arrived, w_gate, preferred_element_type=jnp.float32)
    up_part = jnp.einsum("secd,efd->secf", arrived, w_up, preferred_element_type=jnp.float32)
    activation = (jax.nn.silu(gate_part) * up_part).astype(jnp.bfloat16)
    expert_out = jnp.einsum(
        "secf,efd->secd", activation, w_down, preferred_element_type=jnp.float32
    ).astype(jnp.bfloat16)
    summed = lax.psum_scatter(
        expert_out.astype(jnp.float32).astype(jnp.bfloat16), "half", scatter_dimension=3, tiled=True
    ).astype(jnp.float32)
    returned = lax.all_to_all(
        summed.reshape(ep_count, local_experts * capacity, half_width).astype(jnp.bfloat16),
        "ep",
        split_axis=0,
        concat_axis=0,
        tiled=True,
    ).astype(jnp.float32)
    term = combine_rows(returned.reshape(slot_count, half_width), target, gates)
    expert_sum = lax.psum_scatter(
        term.astype(jnp.bfloat16), "tp", scatter_dimension=1, tiled=True
    ).astype(jnp.float32)
    slice_width = expert_sum.shape[1]
    own_columns = lax.dynamic_slice_in_dim(
        hidden, lax.axis_index("tp") * slice_width, slice_width, 1
    )
    return (own_columns + expert_sum).astype(jnp.bfloat16)


VMEM_BYTES = 60 * 1024 * 1024
LANES = 128
ROW_TILE = 8
MESH = pl.DeviceIdType.MESH


def remote(src, dst, send, recv, **where):
    return pltpu.make_async_remote_copy(
        src_ref=src,
        dst_ref=dst,
        send_sem=send,
        recv_sem=recv,
        device_id=where,
        device_id_type=MESH,
    )


def partner(index, p):
    bit = 1
    while bit <= p:
        if p & bit:
            index = index + bit - 2 * bit * (index // bit % 2)
        bit *= 2
    return index


def each(low, high, body):
    many = 2
    whole = (high - low) // many

    def several(i, carry):
        for k in range(many):
            body(low + i * many + k)
        return carry

    lax.fori_loop(0, whole, several, 0)
    for k in range(low + whole * many, high):
        body(k)


def layer_kernel(
    sizes,
    q_ref,
    nk_ref,
    nv_ref,
    len_ref,
    res_ref,
    gain_ref,
    ids_ref,
    gw_ref,
    ck_hbm,
    cv_hbm,
    ow_hbm,
    wg_hbm,
    wu_hbm,
    wd_hbm,
    out_ref,
    ck,
    cv,
    ow,
    wgu,
    wd,
    att_f,
    att,
    gain,
    table,
    mix_out,
    mix_in,
    own_hidden,
    hid,
    xt,
    squares,
    sums,
    act,
    a_out,
    a_in,
    b_out,
    b_in,
    mine,
    c_out,
    c_in,
    load_sem,
    w_sem,
    att_s,
    att_r,
    gain_s,
    gain_r,
    table_s,
    table_r,
    mix_s,
    mix_r,
    hz_s,
    hz_r,
    hx_s,
    hx_r,
    ht_s,
    ht_r,
    a_s,
    a_r,
    b_s,
    b_r,
    c_s,
    c_r,
):
    n_ep, n_half = sizes["ep"], sizes["half"]
    me_z, me_h, me_t = lax.axis_index("ep"), lax.axis_index("half"), lax.axis_index("tp")
    other = 1 - me_t
    requests, context, head_size = ck.shape
    heads = q_ref.shape[1] // head_size
    local, hidden_units = wgu.shape[0], wgu.shape[1] // 2
    block, piece = res_ref.shape[0], res_ref.shape[1] // 2
    rows = n_ep * block
    width = n_half * 2 * piece

    loads = [
        pltpu.make_async_copy(ck_hbm, ck, load_sem.at[0]),
        pltpu.make_async_copy(cv_hbm, cv, load_sem.at[1]),
        pltpu.make_async_copy(ow_hbm, ow, load_sem.at[2]),
    ]
    for load in loads:
        load.start()

    def weight_copy(k, j):
        if k < 2:
            return pltpu.make_async_copy(
                (wg_hbm, wu_hbm)[k].at[j],
                wgu.at[j, pl.ds(k * hidden_units, hidden_units)],
                w_sem.at[k, j],
            )
        part = pl.ds(j * hidden_units, hidden_units)
        return pltpu.make_async_copy(wd_hbm.at[part], wd.at[part], w_sem.at[k, j])

    def start_weights(kinds, low, high):
        for j in range(low, high):
            for k in kinds:
                weight_copy(k, j).start()

    start_weights((0, 1), 0, local // 2)

    barrier = pltpu.get_barrier_semaphore()
    pl.semaphore_signal(barrier, inc=1, device_id={"tp": other}, device_id_type=MESH)
    for d in range(1, n_half):
        pl.semaphore_signal(
            barrier, inc=1, device_id={"half": lax.rem(me_h + d, n_half)}, device_id_type=MESH
        )
    for p in range(1, n_ep):
        pl.semaphore_signal(barrier, inc=1, device_id={"ep": partner(me_z, p)}, device_id_type=MESH)

    sent = []

    def go(copy):
        copy.start()
        sent.append(copy)
        return copy

    spread = jnp.broadcast_to(len_ref[...].astype(jnp.float32), (LANES, requests)).T

    loads[0].wait()
    loads[1].wait()
    step = ROW_TILE
    scale = 1.0 / math.sqrt(head_size)
    shape = (heads * step, step * context)
    row = lax.broadcasted_iota(jnp.int32, shape, 0)
    column = lax.broadcasted_iota(jnp.int32, shape, 1)
    same = (row % step) == (column // context)
    position = (column % context).astype(jnp.float32)
    for g in range(requests // step):
        part = pl.ds(g * step, step)
        q_all = q_ref[part].astype(jnp.float32)
        q = jnp.concatenate(
            [q_all[:, h * head_size : (h + 1) * head_size] for h in range(heads)], axis=0
        )
        nk = jnp.concatenate([nk_ref[part].astype(jnp.float32)] * heads, axis=0)
        nv = jnp.concatenate([nv_ref[part].astype(jnp.float32)] * heads, axis=0)
        valid = jnp.concatenate([spread[g * step : (g + 1) * step, :1]] * heads, axis=0)
        keys = ck[part].reshape(step * context, head_size)
        values = cv[part].reshape(step * context, head_size)
        scores = (
            lax.dot_general(
                q.astype(jnp.bfloat16),
                keys,
                (((1,), (1,)), ((), ())),
                preferred_element_type=jnp.float32,
            )
            * scale
        )
        own = jnp.sum(q * nk, axis=1, keepdims=True) * scale
        scores = jnp.where(same & (position < valid), scores, -1e30)
        highest = jnp.maximum(jnp.max(scores, axis=1, keepdims=True), own)
        weights = jnp.exp(scores - highest)
        own_weight = jnp.exp(own - highest)
        inverse = 1.0 / (jnp.sum(weights, axis=1, keepdims=True) + own_weight)
        probs = (weights * inverse).astype(jnp.bfloat16)
        own_prob = (own_weight * inverse).astype(jnp.bfloat16).astype(jnp.float32)
        mixture = jnp.dot(probs, values, preferred_element_type=jnp.float32) + own_prob * nv
        for h in range(heads):
            att_f[part, h * head_size : (h + 1) * head_size] = mixture[h * step : (h + 1) * step]
    att[me_h] = att_f[...].astype(jnp.bfloat16)
    gates = gw_ref[...] / jnp.sum(gw_ref[...], axis=0, keepdims=True)
    expert_row = lax.broadcasted_iota(jnp.int32, (table.shape[1], block), 0)
    own_table = jnp.zeros((table.shape[1], block), jnp.float32)
    for k in range(ids_ref.shape[0]):
        own_table += jnp.where(expert_row == ids_ref[k : k + 1, :], gates[k : k + 1, :], 0.0)
    table[0] = own_table
    gain[me_h] = jnp.broadcast_to(gain_ref[...], gain.shape[1:])

    pl.semaphore_wait(barrier, 1 + (n_half - 1) + (n_ep - 1))
    att_copies = [
        go(
            remote(
                att.at[me_h],
                att.at[me_h],
                att_s.at[d],
                att_r.at[d],
                half=lax.rem(me_h + d, n_half),
            )
        )
        for d in range(1, n_half)
    ]
    start_weights((0, 1), local // 2, local * 3 // 4)
    gain_copies = [
        go(
            remote(
                gain.at[me_h],
                gain.at[me_h],
                gain_s.at[d],
                gain_r.at[d],
                half=lax.rem(me_h + d, n_half),
            )
        )
        for d in range(1, n_half)
    ]
    table_copies = [
        go(
            remote(
                table.at[0], table.at[p], table_s.at[p], table_r.at[p], ep=partner(me_z, p)
            )
        )
        for p in range(1, n_ep)
    ]
    loads[2].wait()
    for copy in att_copies:
        copy.wait_recv()

    attended = att[...].reshape(block, att.shape[2])
    other_columns = pl.ds(pl.multiple_of(other * piece, piece), piece)
    my_columns = pl.ds(pl.multiple_of(me_t * piece, piece), piece)
    mix_out[...] = jnp.dot(
        attended, ow[:, other_columns], preferred_element_type=jnp.float32
    ).astype(jnp.bfloat16)
    mix_copy = go(remote(mix_out, mix_in, mix_s, mix_r, tp=other))
    start_weights((0, 1), local * 3 // 4, local)
    mixed = jnp.dot(attended, ow[:, my_columns], preferred_element_type=jnp.float32)
    mixed = mixed + res_ref[:, my_columns].astype(jnp.float32)
    mix_copy.wait_recv()
    hidden = mixed + mix_in[...].astype(jnp.float32)
    own_hidden[...] = hidden
    hid[0, me_h, me_t] = hidden.astype(jnp.bfloat16)

    z_copies = {
        p: go(
            remote(
                hid.at[0, me_h, me_t],
                hid.at[p, me_h, me_t],
                hz_s.at[p],
                hz_r.at[p],
                ep=partner(me_z, p),
            )
        )
        for p in range(1, n_ep)
    }
    x_copies, t_copies = {}, {}

    near, far = range(n_ep // 2), range(n_ep // 2, n_ep)

    def take(group, h, t):
        gain_columns = pl.ds(pl.multiple_of(t * piece, piece), piece)
        scaled = []
        for p in group:
            value = hid[p, h, t].astype(jnp.float32)
            square = value * value
            total = square[:, :LANES]
            for k in range(1, piece // LANES):
                total = total + square[:, k * LANES : (k + 1) * LANES]
            squares[p] += total
            scaled.append(value * gain[h, 0:1, gain_columns])
        columns = pl.ds(pl.multiple_of((h * 2 + t) * piece, piece), piece)
        xt[columns, group[0] * block : (group[-1] + 1) * block] = (
            jnp.concatenate(scaled, axis=0).T.astype(jnp.bfloat16)
        )

    def to_sibling(p, dx, h):
        here = hid.at[p, h, me_t]
        t_copies[p, dx] = go(remote(here, here, ht_s.at[dx, p], ht_r.at[dx, p], tp=other))

    def spread_own(group):
        for p in group:
            if p > 0:
                z_copies[p].wait_recv()
            here = hid.at[p, me_h, me_t]
            for dx in range(1, n_half):
                x_copies[p, dx] = go(
                    remote(
                        here,
                        here,
                        hx_s.at[dx, p],
                        hx_r.at[dx, p],
                        half=lax.rem(me_h + dx, n_half),
                    )
                )
            to_sibling(p, 0, me_h)

    def spread_crossed(group):
        for p in group:
            for dx in range(1, n_half):
                x_copies[p, dx].wait_recv()
                to_sibling(p, dx, lax.rem(me_h - dx + n_half, n_half))

    def product(h, t, j):
        span = pl.ds(pl.multiple_of((h * 2 + t) * piece, piece), piece)
        return jnp.dot(wgu[j, :, span], xt[span, :], preferred_element_type=jnp.float32)

    def finish(h, inverse, j):
        weight = jnp.concatenate(
            [table[p, pl.ds((me_z * 2 + me_t) * local + j, 1), :] for p in range(n_ep)], axis=1
        )
        both = sums[j] + product(h, other, j)
        gate = both[:hidden_units] * inverse
        silu = gate / (1.0 + jnp.exp(jnp.minimum(-gate, 88.0)))
        value = silu * (both[hidden_units:] * (inverse * weight))
        act[:, pl.ds(pl.multiple_of(j * hidden_units, hidden_units), hidden_units)] = value.T.astype(jnp.bfloat16)

    a_copies, b_copies, c_copies = {}, {}, {}

    def down(h, t, store):
        tile = piece // 2

        def one(k, carry):
            columns = pl.ds(pl.multiple_of((h * 2 + t) * piece + k * tile, tile), tile)
            value = jnp.dot(act[...], wd[:, columns], preferred_element_type=jnp.float32)
            store(pl.ds(pl.multiple_of(k * tile, tile), tile), value)
            return carry

        lax.fori_loop(0, 2, one, 0)

    def send_across(dx):
        def store(columns, value):
            a_out[dx, :, columns] = value.astype(jnp.bfloat16)

        down(lax.rem(me_h + dx, n_half), other, store)
        a_copies[dx] = go(remote(a_out.at[dx], a_in.at[dx], a_s.at[dx], a_r.at[dx], tp=other))

    def send_over(dx):
        a_copies[dx].wait_recv()
        total = mine[dx] + a_in[dx].astype(jnp.float32)
        if dx == 0:
            mine[dx] = total
            return
        for p in reversed(range(n_ep)):
            part = pl.ds(p * block, block)
            b_out[dx - 1, part] = total[p * block : (p + 1) * block].astype(jnp.bfloat16)
            b_copies[p, dx] = go(
                remote(
                    b_out.at[dx - 1, part],
                    b_in.at[dx - 1, part],
                    b_s.at[dx, p],
                    b_r.at[dx, p],
                    half=lax.rem(me_h + dx, n_half),
                )
            )

    spread_own(near)
    for copy in gain_copies:
        copy.wait_recv()
    squares[...] = jnp.zeros_like(squares)
    take(near, me_h, me_t)
    spread_own(far)
    take(far, me_h, me_t)
    def first_piece(j):
        weight_copy(0, j).wait()
        weight_copy(1, j).wait()
        weight_copy(2, j).start()
        sums[j] = product(me_h, me_t, j)

    def next_piece(h, t, j):
        sums[j] += product(h, t, j)

    each(0, local // 2, first_piece)
    spread_crossed(near)
    each(local // 2, local, first_piece)
    for group in (near, far):
        for p in group:
            t_copies[p, 0].wait_recv()
        take(group, me_h, other)
    each(0, local // 2, functools.partial(next_piece, me_h, other))
    spread_crossed(far)
    each(local // 2, local, functools.partial(next_piece, me_h, other))
    for copy in table_copies:
        copy.wait_recv()
    for dx in range(1, n_half):
        h = lax.rem(me_h - dx + n_half, n_half)
        take(near, h, me_t)
        take(far, h, me_t)
        each(0, local, functools.partial(next_piece, h, me_t))
        for group in (near, far):
            for p in group:
                t_copies[p, dx].wait_recv()
            take(group, h, other)
        if dx == n_half - 1:
            total = jnp.sum(squares[...].reshape(rows, LANES).T, axis=0, keepdims=True)
            inverse = lax.rsqrt(total / width + EPSILON)
        if dx < n_half - 1:
            each(0, local, functools.partial(next_piece, h, other))
        else:
            each(0, local, functools.partial(finish, h, inverse))
    for j in range(local):
        weight_copy(2, j).wait()
    order = [*range(1, n_half), 0]
    for dx in order:
        send_across(dx)

        def keep(columns, value):
            mine[dx, :, columns] = value

        down(lax.rem(me_h + dx, n_half), me_t, keep)
        send_over(dx)
    for p in reversed(range(n_ep)):
        part = slice(p * block, (p + 1) * block)
        total = mine[0, part]
        for dx in range(1, n_half):
            b_copies[p, dx].wait_recv()
            total = total + b_in[dx - 1, part].astype(jnp.float32)
        if p > 0:
            c_out[p - 1] = total.astype(jnp.bfloat16)
            c_copies[p] = go(
                remote(c_out.at[p - 1], c_in.at[p - 1], c_s.at[p], c_r.at[p], ep=partner(me_z, p))
            )
        else:
            own_hidden[...] += total
    result = own_hidden[...]
    for p in range(1, n_ep):
        c_copies[p].wait_recv()
        result = result + c_in[p - 1].astype(jnp.float32)
    out_ref[...] = result.astype(jnp.bfloat16)
    for copy in sent:
        copy.wait_send()


def on_device(sizes, *args):
    (
        queries,
        new_keys,
        new_values,
        cache_keys,
        cache_values,
        lengths,
        out_weight,
        residual,
        norm_gain,
        expert_ids,
        gate_weights,
        w_gate,
        w_up,
        w_down,
    ) = args
    n_ep, n_half, n_tp = sizes["ep"], sizes["half"], sizes["tp"]
    requests, key_heads, context, head_size = cache_keys.shape
    block, half_width = residual.shape
    local, hidden_units, width = w_gate.shape
    piece = half_width // 2
    rows = n_ep * block
    experts = local * n_ep * n_tp
    bf16, f32 = jnp.bfloat16, jnp.float32
    buffers = [
        ((requests, context, head_size), bf16),
        ((requests, context, head_size), bf16),
        (out_weight.shape, bf16),
        ((local, 2 * hidden_units, width), bf16),
        ((local * hidden_units, width), bf16),
        (queries.shape, f32),
        ((n_half,) + queries.shape, bf16),
        ((n_half, ROW_TILE, half_width), f32),
        ((n_ep, experts, block), f32),
        ((block, piece), bf16),
        ((block, piece), bf16),
        ((block, piece), f32),
        ((n_ep, n_half, n_tp, block, piece), bf16),
        ((width, rows), bf16),
        ((n_ep, block, LANES), f32),
        ((local, 2 * hidden_units, rows), f32),
        ((rows, local * hidden_units), bf16),
        ((n_half, rows, piece), bf16),
        ((n_half, rows, piece), bf16),
        ((n_half - 1, rows, piece), bf16),
        ((n_half - 1, rows, piece), bf16),
        ((n_half, rows, piece), f32),
        ((n_ep - 1, block, piece), bf16),
        ((n_ep - 1, block, piece), bf16),
    ]
    held = sum(math.prod(shape) * jnp.dtype(kind).itemsize for shape, kind in buffers)
    fits = (
        held * 17 // 16 < VMEM_BYTES
        and n_tp == 2
        and n_ep > 1
        and n_ep & (n_ep - 1) == 0
        and key_heads == 1
        and hidden_units % LANES == 0
        and piece % (2 * LANES) == 0
        and n_half > 1
        and rows % (2 * LANES) == 0
        and requests % (2 * ROW_TILE) == 0
        and block == n_half * requests
    )
    if not fits:
        return staged(*args)
    dma = pltpu.SemaphoreType.DMA
    semaphores = [
        dma((3,)),
        dma((3, local)),
        dma((n_half,)),
        dma((n_half,)),
        dma((n_half,)),
        dma((n_half,)),
        dma((n_ep,)),
        dma((n_ep,)),
        dma,
        dma,
        dma((n_ep,)),
        dma((n_ep,)),
        dma((n_half, n_ep)),
        dma((n_half, n_ep)),
        dma((n_half, n_ep)),
        dma((n_half, n_ep)),
        dma((n_half,)),
        dma((n_half,)),
        dma((n_half, n_ep)),
        dma((n_half, n_ep)),
        dma((n_ep,)),
        dma((n_ep,)),
    ]
    vmem = pl.BlockSpec(memory_space=pltpu.VMEM)
    hbm = pl.BlockSpec(memory_space=pl.ANY)
    return pl.pallas_call(
        functools.partial(layer_kernel, dict(ep=n_ep, half=n_half)),
        out_shape=jax.ShapeDtypeStruct((block, piece), bf16),
        in_specs=[vmem] * 8 + [hbm] * 6,
        out_specs=vmem,
        scratch_shapes=[pltpu.VMEM(shape, kind) for shape, kind in buffers] + semaphores,
        compiler_params=pltpu.CompilerParams(
            collective_id=0, has_side_effects=True, vmem_limit_bytes=VMEM_BYTES
        ),
    )(
        queries,
        new_keys,
        new_values,
        lengths.reshape(1, requests),
        residual,
        norm_gain.reshape(1, half_width),
        expert_ids.T,
        gate_weights.T,
        cache_keys.reshape(requests, context, head_size),
        cache_values.reshape(requests, context, head_size),
        out_weight,
        w_gate,
        w_up,
        w_down.reshape(local * hidden_units, width),
    )


def solution(mesh):
    placed = (
        P(("groups", "ep", "half"), "tp"),
        P(("groups", "ep", "half"), "tp"),
        P(("groups", "ep", "half"), "tp"),
        P(("groups", "ep", "half"), "tp", None, None),
        P(("groups", "ep", "half"), "tp", None, None),
        P(("groups", "ep", "half")),
        P("tp", "half"),
        P(("groups", "ep"), "half"),
        P("half"),
        P(("groups", "ep"), None),
        P(("groups", "ep"), None),
        P(("ep", "tp"), "half", None),
        P(("ep", "tp"), "half", None),
        P(("ep", "tp"), "half", None),
    )
    return jax.shard_map(
        functools.partial(on_device, mesh.shape),
        mesh=mesh,
        in_specs=placed,
        out_specs=P(("groups", "ep"), ("half", "tp")),
        check_vma=False,
    )
```
